512 devices in a mesh: rows: 256 (over x, y, z), sub: 2 (over core).
Axes of the slice: x: 4, y: 8, z: 8, core: 2. Of those that a mesh axis runs over, the one named last changes fastest.
Arguments:
- embeddings: float32 [688128, 768], P(('rows', 'sub')), may hold values from -350 to 350, as said below
- test_matrix: float32 [768, 80], replicated, may hold values from -6 to 6
Outputs:
- basis: float32 [688128, 80], P(('rows', 'sub'))
- projected: float32 [80, 768], replicated
The draws below stay inside these ranges and needn't reach their ends.
Inputs may be any that keep to these rules, and one draw needn't show every extreme that they name: `embeddings`: entries are drawn independently within a row; each column, and possibly each row, carries its own scale, and the entries need not be centred.
All inputs are finite; a program needn't handle non-finite values.
Results may differ from the reference program's by a relative error of at most 0.00005.
Values sent between devices are 32-bit elements; how exact they have to be, the bound alone decides.
No kernel may reach another device: no remote copies, remote signals or barrier semaphores. Data moves between devices by JAX's collectives and lax.ppermute only.
A program may use at most 64 MiB of HBM per device.

```python
import math
import jax
import jax.numpy as jnp
from jax import lax

D = 768
RANK = 80
ROWS = 688128


def draw_embeddings(key, part):
    key = jax.random.fold_in(key, 11)
    base_key, column_key = jax.random.split(key, 2)
    column_scale = jnp.exp(jax.random.uniform(column_key, (D,), jnp.float32, 0.0, math.log(10.0)))
    position = jnp.arange(ROWS, dtype=jnp.float32)[:, None] / jnp.float32(ROWS - 1)
    base = jax.random.truncated_normal(base_key, -6.0, 6.0, (ROWS, D), jnp.float32)
    row_scale = 1.0 + 2.0 * position
    values = base * column_scale[None, :] * row_scale
    return values.astype(jnp.float32)


def centred(stream_key, extent, width, bound, kind=jnp.bfloat16):
    return jnp.clip(width * jax.random.normal(stream_key, extent, jnp.float32), -bound, bound).astype(kind)


def setup_inputs(seed: int = 0) -> dict:
    key_list = jax.random.split(jax.random.key(seed), 3)
    embeddings = draw_embeddings(jax.random.fold_in(key_list[2], 71), 0)
    test_matrix = centred(key_list[1], (D, RANK), 1.0, 6.0, jnp.float32)
    return {"embeddings": embeddings, "test_matrix": test_matrix}


HIGH = lax.Precision.HIGHEST

def orthonormal(matrix):
    gram = jnp.dot(matrix.T.astype(jnp.float32), matrix.astype(jnp.float32), precision=HIGH, preferred_element_type=jnp.float32)
    lower = jnp.linalg.cholesky(gram)
    return lax.linalg.triangular_solve(lower, matrix, left_side=False, lower=True, transpose_a=True)

def reference(embeddings, test_matrix):
    sketch = jnp.dot(embeddings.astype(jnp.float32), test_matrix.astype(jnp.float32), precision=HIGH, preferred_element_type=jnp.float32)
    first = orthonormal(sketch)
    spanned = jnp.dot(embeddings.T.astype(jnp.float32), first.astype(jnp.float32), precision=HIGH, preferred_element_type=jnp.float32)
    powered = jnp.dot(embeddings.astype(jnp.float32), spanned.astype(jnp.float32), precision=HIGH, preferred_element_type=jnp.float32)
    second = orthonormal(powered)
    factor = jnp.sqrt(jnp.float32(ROWS))
    basis = second * factor
    projected = jnp.dot(second.T.astype(jnp.float32), embeddings.astype(jnp.float32), precision=HIGH, preferred_element_type=jnp.float32) / factor
    return (basis, projected)
```

```python
import jax
import jax.numpy as jnp
from jax import lax
from jax.sharding import PartitionSpec as P

HIGH = lax.Precision.HIGHEST
SX, SY, SZ = 4, 8, 8


def product(left, right):
    return jnp.dot(left, right, precision=HIGH, preferred_element_type=jnp.float32)


def right_solve(matrix, lower):
    return lax.linalg.triangular_solve(lower, matrix, left_side=False, lower=True, transpose_a=True)


def partner(axis, k):
    pairs = []
    for x in range(SX):
        for y in range(SY):
            for z in range(SZ):
                to = [x, y, z]
                to[axis] ^= k
                pairs.append(((x * SY + y) * SZ + z, (to[0] * SY + to[1]) * SZ + to[2]))
    return pairs


def tree(parts):
    while len(parts) > 1:
        parts = [parts[i] + parts[i + 1] for i in range(0, len(parts), 2)]
    return parts[0]


def exchange(value, axis, size):
    return tree([value] + [lax.ppermute(value, "rows", partner(axis, k)) for k in range(1, size)])


def total(matrix):
    core = lax.axis_index("sub")
    y = lax.axis_index("rows") // SZ % SY
    tiles = matrix.reshape(10, 8, 6, 128).transpose(0, 2, 1, 3).reshape(60, 8, 128)
    tiles = jnp.pad(tiles, ((0, 4), (0, 0), (0, 0))).reshape(2, 8, 32, 128)
    swap = [(0, 1), (1, 0)]
    pick = lambda a, i: lax.dynamic_index_in_dim(a, i, 0, keepdims=False)
    half = pick(tiles, core) + lax.ppermute(pick(tiles, 1 - core), "sub", swap)
    parts = [pick(half, y)]
    for k in range(1, SY):
        parts.append(lax.ppermute(pick(half, y ^ k), "rows", partner(1, k)))
    piece = tree(parts)
    piece = exchange(piece, 2, SZ)
    piece = exchange(piece, 0, SX)
    half = jnp.zeros((8, 32, 128), jnp.float32)
    half = lax.dynamic_update_index_in_dim(half, piece, y, 0)
    for k in range(1, SY):
        half = lax.dynamic_update_index_in_dim(half, lax.ppermute(piece, "rows", partner(1, k)), y ^ k, 0)
    other = lax.ppermute(half, "sub", swap)
    tiles = jnp.where(core == 0, jnp.stack([half, other]), jnp.stack([other, half]))
    tiles = tiles.reshape(64, 8, 128)[:60]
    return tiles.reshape(10, 6, 8, 128).transpose(0, 2, 1, 3).reshape(80, 768)


def local(embeddings, test_matrix):
    row_total = embeddings.shape[0] * lax.axis_size("rows") * lax.axis_size("sub")
    factor = jnp.sqrt(jnp.float32(row_total))
    sketch = product(embeddings, test_matrix)
    image = total(product(sketch.T, embeddings)).T
    lower = jnp.linalg.cholesky(product(test_matrix.T, image))
    spanned = right_solve(image, lower)
    powered = product(embeddings, spanned)
    reach = total(product(powered.T, embeddings))
    gram = product(reach, spanned)
    gram = 0.5 * (gram + gram.T)
    lower = jnp.linalg.cholesky(gram)
    projected = lax.linalg.triangular_solve(lower, reach, left_side=True, lower=True)
    second = right_solve(powered, lower)
    return (second * factor, projected / factor)


def solution(mesh):
    in_specs = (P(("rows", "sub"), None), P())
    out_specs = (P(("rows", "sub"), None), P())
    return jax.shard_map(local, mesh=mesh, in_specs=in_specs, out_specs=out_specs, check_vma=False)
```

```python
import jax
import jax.numpy as jnp
import numpy as np
from jax import lax
from jax.experimental import pallas as pl
from jax.experimental.pallas import tpu as pltpu
from jax.sharding import Mesh, PartitionSpec as P

SX, SY, SZ = 4, 8, 8
D, RANK = 768, 80
BLOCK = 128
NB = D // BLOCK
UPPER = [(a, b) for a in range(NB) for b in range(a + 1, NB)]
PACKED = len(UPPER) * BLOCK
DIAGS = PACKED + NB // 2 * BLOCK
FLAT = 2560
CHUNK = 448


def split(value):
    high = value.astype(jnp.bfloat16)
    rest = value - high.astype(jnp.float32)
    mid = rest.astype(jnp.bfloat16)
    low = (rest - mid.astype(jnp.float32)).astype(jnp.bfloat16)
    return high, mid, low


def dot(left, right):
    return jnp.dot(left, right, preferred_element_type=jnp.float32)


def exact(left, right, dims):
    return lax.dot_general(left, right, (dims, ((), ())), precision=lax.Precision.HIGHEST,
                           preferred_element_type=jnp.float32)


def iota(axis):
    return lax.broadcasted_iota(jnp.int32, (BLOCK, BLOCK), axis)


def gram_kernel(x_ref, flat_ref, even_ref, odd_ref):
    step = pl.program_id(0)
    high, mid, low = split(x_ref[...])
    high_t, mid_t, low_t = high.T, mid.T, low.T
    slot = 0
    for i in range(3):
        rows = slice(256 * i, 256 * (i + 1))
        for j in range(i, 3):
            cols = slice(256 * j, 256 * (j + 1))
            main = dot(high_t[rows], high[:, cols]) + dot(mid_t[rows], mid[:, cols])
            side = dot(high_t[rows], mid[:, cols]) + dot(high_t[rows], low[:, cols])
            if i != j:
                main = main + side + dot(mid_t[rows], high[:, cols]) + dot(low_t[rows], high[:, cols])

            @pl.when(step == 0)
            def _():
                even_ref[slot] = main
                if i == j:
                    odd_ref[i] = side

            @pl.when(step > 0)
            def _():
                even_ref[slot] += main
                if i == j:
                    odd_ref[i] += side
            slot += 1

    @pl.when(step == pl.num_programs(0) - 1)
    def _():
        row, col = iota(0), iota(1)
        slot = 0
        diagonals = []
        for i in range(3):
            for j in range(i, 3):
                value = even_ref[slot]
                slot += 1
                if i == j:
                    value = value + (odd_ref[i] + odd_ref[i].T)
                for p in range(2):
                    for q in range(2):
                        a, b = 2 * i + p, 2 * j + q
                        if a < b:
                            at = UPPER.index((a, b)) * BLOCK
                            flat_ref[at:at + BLOCK, :] = value[p * BLOCK:(p + 1) * BLOCK, q * BLOCK:(q + 1) * BLOCK]
                if i == j:
                    first, second = value[:BLOCK, :BLOCK], value[BLOCK:, BLOCK:]
                    at = PACKED + i * BLOCK
                    flat_ref[at:at + BLOCK, :] = jnp.where(row <= col, first, second)
                    diagonals.append(jnp.sum(jnp.where(row == col, second, 0.0), axis=0, keepdims=True))
        flat_ref[DIAGS:, :] = jnp.zeros((FLAT - DIAGS, BLOCK), jnp.float32)
        for i in range(3):
            flat_ref[DIAGS + i:DIAGS + i + 1, :] = diagonals[i]


def inverse_factor(gram):
    row = lax.broadcasted_iota(jnp.int32, (RANK, RANK), 0)
    col = lax.broadcasted_iota(jnp.int32, (RANK, RANK), 1)
    lane = lax.broadcasted_iota(jnp.int32, (1, RANK), 1)
    state = gram
    for j in range(RANK):
        pivot = state[j:j + 1, :]
        inverse = 1.0 / state[j:j + 1, j:j + 1]
        factor = jnp.where(row[:, :1] > j, state[:, j:j + 1] * inverse, 0.0)
        cleared = jnp.where((col == j) & (row > j), 0.0, state)
        state = cleared - factor * jnp.where(lane == j, 1.0, pivot)
    scale = lax.rsqrt(jnp.sum(jnp.where(row == col, state, 0.0), axis=1, keepdims=True))
    return jnp.where(row > col, state, jnp.where(row == col, 1.0, 0.0)) * scale


def finish_kernel(factor, flat_ref, test_ref, x_hbm, basis_ref, projected_ref, x_ref, c_ref, sem):
    copy = pltpu.make_async_copy(x_hbm, x_ref, sem)
    copy.start()
    row, col = iota(0), iota(1)
    for n, (a, b) in enumerate(UPPER):
        value = flat_ref[n * BLOCK:(n + 1) * BLOCK, :]
        c_ref[a * BLOCK:(a + 1) * BLOCK, b * BLOCK:(b + 1) * BLOCK] = value
        c_ref[b * BLOCK:(b + 1) * BLOCK, a * BLOCK:(a + 1) * BLOCK] = value.T
    for i in range(NB // 2):
        value = flat_ref[PACKED + i * BLOCK:PACKED + (i + 1) * BLOCK, :]
        flipped = value.T
        at = 2 * i * BLOCK
        c_ref[at:at + BLOCK, at:at + BLOCK] = jnp.where(row <= col, value, flipped)
        at += BLOCK
        other = jnp.where(row > col, value, flipped)
        c_ref[at:at + BLOCK, at:at + BLOCK] = jnp.where(row == col, flat_ref[DIAGS + i:DIAGS + i + 1, :], other)
    test = test_ref[...]
    image = exact(c_ref[...], test, ((1,), (0,)))
    first = inverse_factor(exact(test, image, ((0,), (0,))))
    spanned = exact(image, first, ((1,), (1,)))
    reach = exact(c_ref[...], spanned, ((1,), (0,)))
    second = inverse_factor(exact(spanned, reach, ((0,), (0,))))
    projected_ref[...] = exact(second, reach, ((1,), (1,))) / factor
    weight = exact(spanned, second, ((1,), (1,))) * factor
    copy.wait()
    basis_ref[...] = exact(x_ref[...], weight, ((1,), (0,)))


def tree(parts):
    while len(parts) > 1:
        parts = [parts[i] + parts[i + 1] for i in range(0, len(parts), 2)]
    return parts[0]


def everyone(value, axis, size):
    return lax.all_to_all(jnp.broadcast_to(value, (size,) + value.shape), axis, 0, 0)


def pick(array, i):
    return lax.dynamic_index_in_dim(array, i, 0, keepdims=False)


def stacked_sum(values):
    return tree([values[i] for i in range(values.shape[0])])


def total(flat):
    core = lax.axis_index("core")
    swap = [(0, 1), (1, 0)]
    halves = flat.reshape(2, FLAT // 2, BLOCK)
    value = pick(halves, core) + lax.ppermute(pick(halves, 1 - core), "core", swap)
    value = stacked_sum(lax.all_to_all(value.reshape(SX, -1, BLOCK), "x", 0, 0))
    value = stacked_sum(lax.all_to_all(value.reshape(SY, -1, BLOCK), "y", 0, 0))
    value = stacked_sum(everyone(value, "z", SZ))
    value = everyone(value, "y", SY).reshape(-1, BLOCK)
    value = everyone(value, "x", SX).reshape(-1, BLOCK)
    other = lax.ppermute(value, "core", swap)
    low = jnp.where(core == 0, value, other)
    high = jnp.where(core == 0, other, value)
    return jnp.concatenate([low, high])


def local(embeddings, test_matrix):
    rows = embeddings.shape[0]
    factor = float(np.sqrt(np.float32(rows * 2 * SX * SY * SZ)))
    flat = pl.pallas_call(
        gram_kernel,
        grid=(rows // CHUNK,),
        in_specs=[pl.BlockSpec((CHUNK, D), lambda i: (i, 0))],
        out_specs=pl.BlockSpec((FLAT, BLOCK), lambda i: (0, 0)),
        out_shape=jax.ShapeDtypeStruct((FLAT, BLOCK), jnp.float32),
        scratch_shapes=[pltpu.VMEM((6, 256, 256), jnp.float32), pltpu.VMEM((3, 256, 256), jnp.float32)],
        compiler_params=pltpu.CompilerParams(vmem_limit_bytes=32 * 2 ** 20),
        cost_estimate=pl.CostEstimate(flops=2 * rows * D * D * 4, bytes_accessed=4 * rows * D, transcendentals=0),
    )(embeddings)
    flat = total(flat)
    return pl.pallas_call(
        lambda *refs: finish_kernel(factor, *refs),
        in_specs=[pl.BlockSpec(memory_space=pltpu.VMEM)] * 2 + [pl.BlockSpec(memory_space=pl.ANY)],
        out_specs=[pl.BlockSpec(memory_space=pltpu.VMEM)] * 2,
        out_shape=[jax.ShapeDtypeStruct((rows, RANK), jnp.float32), jax.ShapeDtypeStruct((RANK, D), jnp.float32)],
        scratch_shapes=[pltpu.VMEM((rows, D), jnp.float32), pltpu.VMEM((D, D), jnp.float32), pltpu.SemaphoreType.DMA],
        compiler_params=pltpu.CompilerParams(vmem_limit_bytes=48 * 2 ** 20),
        cost_estimate=pl.CostEstimate(flops=2 * rows * D * RANK * 8, bytes_accessed=4 * rows * D, transcendentals=0),
    )(flat, test_matrix, embeddings)


def solution(mesh):
    grid = Mesh(mesh.devices.reshape(SX, SY, SZ, 2), ("x", "y", "z", "core"))
    in_specs = (P(("x", "y", "z", "core"), None), P())
    out_specs = (P(("x", "y", "z", "core"), None), P())
    return jax.shard_map(local, mesh=grid, in_specs=in_specs, out_specs=out_specs, check_vma=False)
```

```python
import jax
import jax.numpy as jnp
import numpy as np
from jax import lax
from jax.experimental import pallas as pl
from jax.experimental.pallas import tpu as pltpu
from jax.sharding import Mesh, PartitionSpec as P

SX, SY, SZ = 4, 8, 8
D, RANK = 768, 80
BLOCK = 128
NB = D // BLOCK
UPPER = [(a, b) for a in range(NB) for b in range(a + 1, NB)]
PACKED = len(UPPER) * BLOCK
DIAGS = PACKED + NB // 2 * BLOCK
FLAT = 2560
CHUNK, DEEP = 448, 512


def split(value):
    high = value.astype(jnp.bfloat16)
    rest = value - high.astype(jnp.float32)
    mid = rest.astype(jnp.bfloat16)
    low = (rest - mid.astype(jnp.float32)).astype(jnp.bfloat16)
    return high, mid, low


def halves(value):
    high = value.astype(jnp.bfloat16)
    return high, (value - high.astype(jnp.float32)).astype(jnp.bfloat16)


def dot(left, right, dim=0):
    return lax.dot_general(left, right, (((1,), (dim,)), ((), ())), preferred_element_type=jnp.float32)


def iota(axis):
    return lax.broadcasted_iota(jnp.int32, (BLOCK, BLOCK), axis)


def gram_kernel(x_ref, flat_ref, high_ref, mid_ref, even_ref, odd_ref):
    step = pl.program_id(0)

    @pl.when(step == 0)
    def _():
        for ref in (high_ref, mid_ref):
            ref[CHUNK:, :] = jnp.zeros((DEEP - CHUNK, D), jnp.bfloat16)
        even_ref[...] = jnp.zeros(even_ref.shape, jnp.float32)
        odd_ref[...] = jnp.zeros(odd_ref.shape, jnp.float32)

    high_ref[:CHUNK, :], mid_ref[:CHUNK, :] = halves(x_ref[...])
    slot = 0
    for i in range(3):
        rows = slice(256 * i, 256 * (i + 1))
        high_t = high_ref[:, rows].T
        if i < 2:
            mid_t = mid_ref[:, rows].T
        for j in range(i, 3):
            cols = slice(256 * j, 256 * (j + 1))
            if i == j:
                even_ref[slot] += dot(high_t, high_ref[:, cols])
                odd_ref[i] += dot(high_t, mid_ref[:, cols])
            else:
                even_ref[slot] += (dot(high_t, high_ref[:, cols]) + dot(high_t, mid_ref[:, cols])
                                   + dot(mid_t, high_ref[:, cols]))
            slot += 1

    @pl.when(step == pl.num_programs(0) - 1)
    def _():
        row, col = iota(0), iota(1)
        slot = 0
        diagonals = []
        for i in range(3):
            for j in range(i, 3):
                value = even_ref[slot]
                slot += 1
                if i == j:
                    value = value + (odd_ref[i] + odd_ref[i].T)
                for p in range(2):
                    for q in range(2):
                        a, b = 2 * i + p, 2 * j + q
                        if a < b:
                            at = UPPER.index((a, b)) * BLOCK
                            flat_ref[at:at + BLOCK, :] = value[p * BLOCK:(p + 1) * BLOCK, q * BLOCK:(q + 1) * BLOCK]
                if i == j:
                    first, second = value[:BLOCK, :BLOCK], value[BLOCK:, BLOCK:]
                    at = PACKED + i * BLOCK
                    flat_ref[at:at + BLOCK, :] = jnp.where(row <= col, first, second)
                    diagonals.append(jnp.sum(jnp.where(row == col, second, 0.0), axis=0, keepdims=True))
        flat_ref[DIAGS:, :] = jnp.zeros((FLAT - DIAGS, BLOCK), jnp.float32)
        for i in range(3):
            flat_ref[DIAGS + i:DIAGS + i + 1, :] = diagonals[i]


def inverse_factor(gram, beside):
    groups = RANK // 8
    lane = lax.broadcasted_iota(jnp.int32, (1, RANK), 1)
    sub = lax.broadcasted_iota(jnp.int32, (8, RANK), 0)
    state = [gram[8 * g:8 * g + 8, :] for g in range(groups)]
    scales = []
    for g in range(groups):
        at = 8 * g
        columns = [[jnp.broadcast_to(state[h][:, at + k:at + k + 1], (8, RANK)) for k in range(8)] for h in range(g, groups)]
        head = columns[0]
        own = state[g]
        pivots = jnp.zeros((8, RANK), jnp.float32)
        rows, inverses = [], []
        for k in range(8):
            pivot = head[k][k:k + 1, :]
            inverse = 1.0 / pivot
            inverses.append(inverse)
            pivots = jnp.where(sub == k, pivot, pivots)
            line = jnp.where(lane == at + k, 1.0, own[k:k + 1, :])
            rows.append(line)
            factor = jnp.where(sub > k, head[k] * inverse, 0.0)
            for m in range(k + 1, 8):
                head[m] = head[m] - factor * head[m][k:k + 1, :]
            own = jnp.where((sub > k) & (lane == at + k), 0.0, own) - factor * line
        state[g] = own
        scales.append(lax.rsqrt(pivots))
        rows = [jnp.where((lane > at + k) & (lane < at + 8), 0.0, rows[k]) for k in range(8)]
        inside = (lane >= at) & (lane < at + 8)
        for h in range(g + 1, groups):
            below = columns[h - g]
            value = jnp.where(inside, 0.0, state[h])
            for k in range(8):
                factor = below[k] * inverses[k]
                for m in range(k + 1, 8):
                    below[m] = below[m] - factor * head[m][k:k + 1, :]
                value = value - factor * rows[k]
            state[h] = value
        beside(g)
    result = []
    for g in range(groups):
        value = jnp.where(lane < 8 * g + sub, state[g], jnp.where(lane == 8 * g + sub, 1.0, 0.0))
        result.append(value * scales[g])
    return jnp.concatenate(result, axis=0)


def stack(value):
    return jnp.concatenate(split(value), axis=0)


def times(stacked, parts, dim=0):
    high, mid, low = parts
    n = RANK
    first, second, third = dot(stacked, high, dim), dot(stacked[:2 * n], mid, dim), dot(stacked[:n], low, dim)
    small = first[2 * n:] + second[n:] + third
    return first[:n] + (first[n:2 * n] + second[:n] + small)


def finish_kernel(factor, flat_ref, test_ref, x_hbm, basis_ref, projected_ref, x_ref, c_ref, parts_ref, sem):
    copy = pltpu.make_async_copy(x_hbm, x_ref, sem)
    copy.start()
    row, col = iota(0), iota(1)

    def place(a, b, value):
        for k, part in enumerate(split(value)):
            c_ref[k, a * BLOCK:(a + 1) * BLOCK, b * BLOCK:(b + 1) * BLOCK] = part

    for n, (a, b) in enumerate(UPPER):
        value = flat_ref[n * BLOCK:(n + 1) * BLOCK, :]
        place(a, b, value)
        place(b, a, value.T)
    for i in range(NB // 2):
        value = flat_ref[PACKED + i * BLOCK:PACKED + (i + 1) * BLOCK, :]
        flipped = value.T
        place(2 * i, 2 * i, jnp.where(row <= col, value, flipped))
        other = jnp.where(row > col, value, flipped)
        place(2 * i + 1, 2 * i + 1, jnp.where(row == col, flat_ref[DIAGS + i:DIAGS + i + 1, :], other))

    def part_rows(start, size):
        at = slice(start, start + size)
        parts_ref[0, at, :], parts_ref[1, at, :] = halves(x_ref[at, :])

    covariance = [c_ref.at[k] for k in range(3)]
    test = stack(test_ref[...])
    image = times(test, [part[...] for part in covariance])
    gram = times(test, split(image), 1)
    copy.wait()
    first = inverse_factor(gram, lambda g: part_rows(128 * g, 128))
    spanned = times(stack(first), split(image))
    spanned_stack = stack(spanned)
    reach = times(spanned_stack, [part[...] for part in covariance])
    gram = times(spanned_stack, split(reach), 1)
    done = 128 * (RANK // 8)
    second = inverse_factor(gram, lambda g: part_rows(done, x_ref.shape[0] - done) if g == 0 else None)
    second_stack = stack(second)
    projected_ref[...] = times(second_stack, split(reach)) * (1.0 / factor)
    weight = jnp.concatenate(halves(times(second_stack, split(spanned)) * factor), axis=0)
    main, rest = dot(weight, parts_ref[0], 1), dot(weight, parts_ref[1], 1)
    basis_ref[...] = main[:RANK] + (main[RANK:] + rest[:RANK] + rest[RANK:])


def tree(parts):
    while len(parts) > 1:
        parts = [parts[i] + parts[i + 1] for i in range(0, len(parts), 2)]
    return parts[0]


def everyone(value, axis, size):
    return lax.all_to_all(jnp.broadcast_to(value, (size,) + value.shape), axis, 0, 0)


def pick(array, i):
    return lax.dynamic_index_in_dim(array, i, 0, keepdims=False)


def stacked_sum(values):
    return tree([values[i] for i in range(values.shape[0])])


def total(flat):
    core = lax.axis_index("core")
    swap = [(0, 1), (1, 0)]
    pair = flat.reshape(2, FLAT // 2, BLOCK)
    value = pick(pair, core) + lax.ppermute(pick(pair, 1 - core), "core", swap)
    value = stacked_sum(lax.all_to_all(value.reshape(SX, -1, BLOCK), "x", 0, 0))
    value = stacked_sum(lax.all_to_all(value.reshape(SY, -1, BLOCK), "y", 0, 0))
    value = stacked_sum(everyone(value, "z", SZ))
    value = everyone(value, "y", SY).reshape(-1, BLOCK)
    value = everyone(value, "x", SX).reshape(-1, BLOCK)
    other = lax.ppermute(value, "core", swap)
    low = jnp.where(core == 0, value, other)
    high = jnp.where(core == 0, other, value)
    return jnp.concatenate([low, high])


def local(embeddings, test_matrix):
    rows = embeddings.shape[0]
    factor = float(np.sqrt(np.float32(rows * 2 * SX * SY * SZ)))
    flat = pl.pallas_call(
        gram_kernel,
        grid=(rows // CHUNK,),
        in_specs=[pl.BlockSpec((CHUNK, D), lambda i: (i, 0))],
        out_specs=pl.BlockSpec((FLAT, BLOCK), lambda i: (0, 0)),
        out_shape=jax.ShapeDtypeStruct((FLAT, BLOCK), jnp.float32),
        scratch_shapes=[pltpu.VMEM((DEEP, D), jnp.bfloat16)] * 2
        + [pltpu.VMEM((6, 256, 256), jnp.float32), pltpu.VMEM((3, 256, 256), jnp.float32)],
        compiler_params=pltpu.CompilerParams(vmem_limit_bytes=60 * 2 ** 20),
        cost_estimate=pl.CostEstimate(flops=2 * rows * D * D * 2, bytes_accessed=4 * rows * D, transcendentals=0),
    )(embeddings)
    flat = total(flat)
    basis, projected = pl.pallas_call(
        lambda *refs: finish_kernel(factor, *refs),
        in_specs=[pl.BlockSpec(memory_space=pltpu.VMEM)] * 2 + [pl.BlockSpec(memory_space=pl.ANY)],
        out_specs=[pl.BlockSpec(memory_space=pltpu.VMEM)] * 2,
        out_shape=[jax.ShapeDtypeStruct((RANK, rows), jnp.float32), jax.ShapeDtypeStruct((RANK, D), jnp.float32)],
        scratch_shapes=[
            pltpu.VMEM((rows, D), jnp.float32),
            pltpu.VMEM((3, D, D), jnp.bfloat16),
            pltpu.VMEM((2, rows, D), jnp.bfloat16),
            pltpu.SemaphoreType.DMA,
        ],
        compiler_params=pltpu.CompilerParams(vmem_limit_bytes=48 * 2 ** 20),
        cost_estimate=pl.CostEstimate(flops=2 * rows * D * RANK * 8, bytes_accessed=4 * rows * D, transcendentals=0),
    )(flat, test_matrix.T, embeddings)
    return basis.T, projected


def solution(mesh):
    grid = Mesh(mesh.devices.reshape(SX, SY, SZ, 2), ("x", "y", "z", "core"))
    in_specs = (P(("x", "y", "z", "core"), None), P())
    out_specs = (P(("x", "y", "z", "core"), None), P())
    return jax.shard_map(local, mesh=grid, in_specs=in_specs, out_specs=out_specs, check_vma=False)
```

```python
import jax
import jax.numpy as jnp
import numpy as np
from jax import lax
from jax.experimental import pallas as pl
from jax.experimental.pallas import tpu as pltpu
from jax.sharding import Mesh, PartitionSpec as P

SX, SY, SZ = 4, 8, 8
D, RANK = 768, 80
BLOCK = 128
NB = D // BLOCK
UPPER = [(a, b) for a in range(NB) for b in range(a + 1, NB)]
PACKED = len(UPPER) * BLOCK
DIAGS = PACKED + NB // 2 * BLOCK
FLAT = 2560
CHUNKS = ((0, 512), (512, 512), (1024, 320))


def split(value):
    high = value.astype(jnp.bfloat16)
    rest = value - high.astype(jnp.float32)
    mid = rest.astype(jnp.bfloat16)
    low = (rest - mid.astype(jnp.float32)).astype(jnp.bfloat16)
    return high, mid, low


def halves(value):
    high = value.astype(jnp.bfloat16)
    return high, (value - high.astype(jnp.float32)).astype(jnp.bfloat16)


def dot(left, right, dim=0):
    return lax.dot_general(left, right, (((1,), (dim,)), ((), ())), preferred_element_type=jnp.float32)


def iota(axis):
    return lax.broadcasted_iota(jnp.int32, (BLOCK, BLOCK), axis)


def gram_kernel(x_hbm, flat_ref, x_ref, high_ref, mid_ref, even_ref, odd_ref, sem):
    copies = []
    for n, (start, size) in enumerate(CHUNKS):
        at = pl.ds(start, size)
        copies.append(pltpu.make_async_copy(x_hbm.at[at, :], x_ref.at[at, :], sem.at[n]))
        copies[-1].start()
    used = x_ref.shape[0]
    for ref in (high_ref, mid_ref):
        ref[used:, :] = jnp.zeros((ref.shape[0] - used, D), jnp.bfloat16)

    def products(n):
        start, size = CHUNKS[n]
        deep = slice(start, start + (size + 127) // 128 * 128)
        for i in range(3):
            high_t = high_ref[deep, 256 * i:256 * (i + 1)].T
            for j in range(3):
                cols = slice(256 * j, 256 * (j + 1))
                if i <= j:
                    value = dot(high_t, high_ref[deep, cols])
                    even_ref[3 * i + j] = value if n == 0 else even_ref[3 * i + j] + value
                value = dot(high_t, mid_ref[deep, cols])
                odd_ref[3 * i + j] = value if n == 0 else odd_ref[3 * i + j] + value

    for n, (start, size) in enumerate(CHUNKS):
        copies[n].wait()
        at = slice(start, start + size)
        high_ref[at, :], mid_ref[at, :] = halves(x_ref[at, :])
        if n:
            products(n - 1)
    products(len(CHUNKS) - 1)

    row, col = iota(0), iota(1)
    flat_ref[DIAGS:, :] = jnp.zeros((FLAT - DIAGS, BLOCK), jnp.float32)
    for i in range(3):
        for j in range(i, 3):
            value = even_ref[3 * i + j] + (odd_ref[3 * i + j] + odd_ref[3 * j + i].T)
            for p in range(2):
                for q in range(2):
                    a, b = 2 * i + p, 2 * j + q
                    if a < b:
                        at = UPPER.index((a, b)) * BLOCK
                        flat_ref[at:at + BLOCK, :] = value[p * BLOCK:(p + 1) * BLOCK, q * BLOCK:(q + 1) * BLOCK]
            if i == j:
                first, second = value[:BLOCK, :BLOCK], value[BLOCK:, BLOCK:]
                at = PACKED + i * BLOCK
                flat_ref[at:at + BLOCK, :] = jnp.where(row <= col, first, second)
                flat_ref[DIAGS + i:DIAGS + i + 1, :] = jnp.sum(jnp.where(row == col, second, 0.0), axis=0, keepdims=True)


def inverse_factor(gram, beside):
    groups, shape = RANK // 8, (8, RANK)
    lane = lax.broadcasted_iota(jnp.int32, shape, 1)
    sub = lax.broadcasted_iota(jnp.int32, shape, 0)
    state = [gram[8 * g:8 * g + 8, :] for g in range(groups)]
    scales = []
    for g in range(groups):
        at = 8 * g
        spread = [[jnp.broadcast_to(state[h][:, at + k:at + k + 1], shape) for k in range(8)] for h in range(g, groups)]
        block = [[jnp.broadcast_to(spread[0][j][i:i + 1, :], shape) if i <= j else None for j in range(8)] for i in range(8)]
        lines = [jnp.broadcast_to(state[g][k:k + 1, :], shape) for k in range(8)]
        own, pivots, inverses, rows = state[g], block[0][0], [], []
        for k in range(8):
            inverse = 1.0 / block[k][k]
            inverses.append(inverse)
            unit = jnp.where(lane == at + k, 1.0, lines[k])
            rows.append(jnp.where((lane > at + k) & (lane < at + 8), 0.0, unit))
            for m in range(k + 1, 8):
                factor = block[k][m] * inverse
                for n in range(m, 8):
                    block[m][n] = block[m][n] - factor * block[k][n]
                lines[m] = jnp.where(lane == at + k, 0.0, lines[m]) - factor * unit
            if k:
                own = jnp.where(sub == k, lines[k], own)
                pivots = jnp.where(sub == k, block[k][k], pivots)
        state[g] = own
        scales.append(lax.rsqrt(pivots))
        inside = (lane >= at) & (lane < at + 8)
        for h in range(g + 1, groups):
            below = spread[h - g]
            value = jnp.where(inside, 0.0, state[h])
            for k in range(8):
                factor = below[k] * inverses[k]
                for m in range(k + 1, 8):
                    below[m] = below[m] - factor * block[k][m]
                value = value - factor * rows[k]
            state[h] = value
        beside(g)
    result = []
    for g in range(groups):
        value = jnp.where(lane < 8 * g + sub, state[g], jnp.where(lane == 8 * g + sub, 1.0, 0.0))
        result.append(value * scales[g])
    return jnp.concatenate(result, axis=0)


def stack(value):
    return jnp.concatenate(split(value), axis=0)


def times(stacked, parts, dim=0):
    high, mid, low = parts
    n = RANK
    first, second, third = dot(stacked, high, dim), dot(stacked[:2 * n], mid, dim), dot(stacked[:n], low, dim)
    small = first[2 * n:] + second[n:] + third
    return first[:n] + (first[n:2 * n] + second[:n] + small)


def finish_kernel(factor, flat_ref, test_ref, x_hbm, basis_ref, projected_ref, x_ref, c_ref, parts_ref, sem):
    copy = pltpu.make_async_copy(x_hbm, x_ref, sem)
    copy.start()
    row, col = iota(0), iota(1)

    def place(a, b, value):
        for k, part in enumerate(split(value)):
            c_ref[k, a * BLOCK:(a + 1) * BLOCK, b * BLOCK:(b + 1) * BLOCK] = part

    for n, (a, b) in enumerate(UPPER):
        value = flat_ref[n * BLOCK:(n + 1) * BLOCK, :]
        place(a, b, value)
        place(b, a, value.T)
    for i in range(NB // 2):
        value = flat_ref[PACKED + i * BLOCK:PACKED + (i + 1) * BLOCK, :]
        flipped = value.T
        place(2 * i, 2 * i, jnp.where(row <= col, value, flipped))
        other = jnp.where(row > col, value, flipped)
        place(2 * i + 1, 2 * i + 1, jnp.where(row == col, flat_ref[DIAGS + i:DIAGS + i + 1, :], other))

    def part_rows(start, size):
        at = slice(start, start + size)
        parts_ref[0, at, :], parts_ref[1, at, :] = halves(x_ref[at, :])

    covariance = [c_ref.at[k] for k in range(3)]
    test = stack(test_ref[...])
    image = times(test, [part[...] for part in covariance])
    gram = times(test, split(image), 1)
    copy.wait()
    first = inverse_factor(gram, lambda g: part_rows(128 * g, 128))
    spanned = times(stack(first), split(image))
    spanned_stack = stack(spanned)
    reach = times(spanned_stack, [part[...] for part in covariance])
    gram = times(spanned_stack, split(reach), 1)
    done = 128 * (RANK // 8)
    second = inverse_factor(gram, lambda g: part_rows(done, x_ref.shape[0] - done) if g == 0 else None)
    second_stack = stack(second)
    projected_ref[...] = times(second_stack, split(reach)) * (1.0 / factor)
    weight = jnp.concatenate(halves(times(second_stack, split(spanned)) * factor), axis=0)
    main, rest = dot(weight, parts_ref[0], 1), dot(weight, parts_ref[1], 1)
    basis_ref[...] = main[:RANK] + (main[RANK:] + rest[:RANK] + rest[RANK:])


def tree(parts):
    while len(parts) > 1:
        parts = [parts[i] + parts[i + 1] for i in range(0, len(parts), 2)]
    return parts[0]


def everyone(value, axis, size):
    return lax.all_to_all(jnp.broadcast_to(value, (size,) + value.shape), axis, 0, 0)


def pick(array, i):
    return lax.dynamic_index_in_dim(array, i, 0, keepdims=False)


def stacked_sum(values):
    return tree([values[i] for i in range(values.shape[0])])


def total(flat):
    core = lax.axis_index("core")
    swap = [(0, 1), (1, 0)]
    pair = flat.reshape(2, FLAT // 2, BLOCK)
    value = pick(pair, core) + lax.ppermute(pick(pair, 1 - core), "core", swap)
    value = stacked_sum(lax.all_to_all(value.reshape(SX, -1, BLOCK), "x", 0, 0))
    value = stacked_sum(lax.all_to_all(value.reshape(SY, -1, BLOCK), "y", 0, 0))
    value = stacked_sum(everyone(value, "z", SZ))
    value = everyone(value, "y", SY).reshape(-1, BLOCK)
    value = everyone(value, "x", SX).reshape(-1, BLOCK)
    other = lax.ppermute(value, "core", swap)
    low = jnp.where(core == 0, value, other)
    high = jnp.where(core == 0, other, value)
    return jnp.concatenate([low, high])


def local(embeddings, test_matrix):
    rows = embeddings.shape[0]
    factor = float(np.sqrt(np.float32(rows * 2 * SX * SY * SZ)))
    flat = pl.pallas_call(
        gram_kernel,
        in_specs=[pl.BlockSpec(memory_space=pl.ANY)],
        out_specs=pl.BlockSpec(memory_space=pltpu.VMEM),
        out_shape=jax.ShapeDtypeStruct((FLAT, BLOCK), jnp.float32),
        scratch_shapes=[pltpu.VMEM((rows, D), jnp.float32)]
        + [pltpu.VMEM((CHUNKS[-1][0] + 512, D), jnp.bfloat16)] * 2
        + [pltpu.VMEM((9, 256, 256), jnp.float32)] * 2
        + [pltpu.SemaphoreType.DMA((len(CHUNKS),))],
        compiler_params=pltpu.CompilerParams(vmem_limit_bytes=50 * 2 ** 20),
        cost_estimate=pl.CostEstimate(flops=2 * rows * D * D * 2, bytes_accessed=4 * rows * D, transcendentals=0),
    )(embeddings)
    flat = total(flat)
    basis, projected = pl.pallas_call(
        lambda *refs: finish_kernel(factor, *refs),
        in_specs=[pl.BlockSpec(memory_space=pltpu.VMEM)] * 2 + [pl.BlockSpec(memory_space=pl.ANY)],
        out_specs=[pl.BlockSpec(memory_space=pltpu.VMEM)] * 2,
        out_shape=[jax.ShapeDtypeStruct((RANK, rows), jnp.float32), jax.ShapeDtypeStruct((RANK, D), jnp.float32)],
        scratch_shapes=[
            pltpu.VMEM((rows, D), jnp.float32),
            pltpu.VMEM((3, D, D), jnp.bfloat16),
            pltpu.VMEM((2, rows, D), jnp.bfloat16),
            pltpu.SemaphoreType.DMA,
        ],
        compiler_params=pltpu.CompilerParams(vmem_limit_bytes=50 * 2 ** 20),
        cost_estimate=pl.CostEstimate(flops=2 * rows * D * RANK * 8, bytes_accessed=4 * rows * D, transcendentals=0),
    )(flat, test_matrix.T, embeddings)
    return basis.T, projected


def solution(mesh):
    grid = Mesh(mesh.devices.reshape(SX, SY, SZ, 2), ("x", "y", "z", "core"))
    in_specs = (P(("x", "y", "z", "core"), None), P())
    out_specs = (P(("x", "y", "z", "core"), None), P())
    return jax.shard_map(local, mesh=grid, in_specs=in_specs, out_specs=out_specs, check_vma=False)
```

```python
import jax
import jax.numpy as jnp
import numpy as np
from jax import lax
from jax.experimental import pallas as pl
from jax.experimental.pallas import tpu as pltpu
from jax.sharding import Mesh, PartitionSpec as P

SX, SY, SZ = 4, 8, 8
D, RANK = 768, 80
BLOCK = 128
NB = D // BLOCK
UPPER = [(a, b) for a in range(NB) for b in range(a + 1, NB)]
PACKED = len(UPPER) * BLOCK
DIAGS = PACKED + NB // 2 * BLOCK
FLAT = 2560
CHUNKS = ((0, 512), (512, 512), (1024, 320))


def split(value):
    high = value.astype(jnp.bfloat16)
    rest = value - high.astype(jnp.float32)
    mid = rest.astype(jnp.bfloat16)
    low = (rest - mid.astype(jnp.float32)).astype(jnp.bfloat16)
    return high, mid, low


def halves(value):
    high = value.astype(jnp.bfloat16)
    return high, (value - high.astype(jnp.float32)).astype(jnp.bfloat16)


def dot(left, right, dim=0):
    return lax.dot_general(left, right, (((1,), (dim,)), ((), ())), preferred_element_type=jnp.float32)


def iota(axis):
    return lax.broadcasted_iota(jnp.int32, (BLOCK, BLOCK), axis)


def gram_kernel(x_hbm, flat_ref, x_ref, high_ref, mid_ref, even_ref, odd_ref, sem):
    copies = []
    for n, (start, size) in enumerate(CHUNKS):
        at = pl.ds(start, size)
        copies.append(pltpu.make_async_copy(x_hbm.at[at, :], x_ref.at[at, :], sem.at[n]))
        copies[-1].start()
    used = x_ref.shape[0]
    for ref in (high_ref, mid_ref):
        ref[used:, :] = jnp.zeros((ref.shape[0] - used, D), jnp.bfloat16)

    def products(n):
        start, size = CHUNKS[n]
        deep = slice(start, start + (size + 127) // 128 * 128)
        for i in range(3):
            high_t = high_ref[deep, 256 * i:256 * (i + 1)].T
            for j in range(3):
                cols = slice(256 * j, 256 * (j + 1))
                if i <= j:
                    value = dot(high_t, high_ref[deep, cols])
                    even_ref[3 * i + j] = value if n == 0 else even_ref[3 * i + j] + value
                value = dot(high_t, mid_ref[deep, cols])
                odd_ref[3 * i + j] = value if n == 0 else odd_ref[3 * i + j] + value

    for n, (start, size) in enumerate(CHUNKS):
        copies[n].wait()
        at = slice(start, start + size)
        high_ref[at, :], mid_ref[at, :] = halves(x_ref[at, :])
        if n:
            products(n - 1)
    products(len(CHUNKS) - 1)

    row, col = iota(0), iota(1)
    flat_ref[DIAGS:, :] = jnp.zeros((FLAT - DIAGS, BLOCK), jnp.float32)
    for i in range(3):
        for j in range(i, 3):
            value = even_ref[3 * i + j] + (odd_ref[3 * i + j] + odd_ref[3 * j + i].T)
            for p in range(2):
                for q in range(2):
                    a, b = 2 * i + p, 2 * j + q
                    if a < b:
                        at = UPPER.index((a, b)) * BLOCK
                        flat_ref[at:at + BLOCK, :] = value[p * BLOCK:(p + 1) * BLOCK, q * BLOCK:(q + 1) * BLOCK]
            if i == j:
                first, second = value[:BLOCK, :BLOCK], value[BLOCK:, BLOCK:]
                at = PACKED + i * BLOCK
                flat_ref[at:at + BLOCK, :] = jnp.where(row <= col, first, second)
                flat_ref[DIAGS + i:DIAGS + i + 1, :] = jnp.sum(jnp.where(row == col, second, 0.0), axis=0, keepdims=True)


def inverse_factor(gram, beside):
    groups, shape = RANK // 8, (8, RANK)
    lane = lax.broadcasted_iota(jnp.int32, shape, 1)
    sub = lax.broadcasted_iota(jnp.int32, shape, 0)
    state = [gram[8 * g:8 * g + 8, :] for g in range(groups)]
    diagonal = [jnp.where(lane == 8 * g + sub, state[g], 0.0) for g in range(groups)]
    along = lax.rsqrt(jnp.sum(sum(diagonal[1:], diagonal[0]), axis=0, keepdims=True))
    state = [state[g] * lax.rsqrt(jnp.sum(diagonal[g], axis=1, keepdims=True)) * along for g in range(groups)]

    def column(h, j):
        return jnp.broadcast_to(state[h][:, j:j + 1], shape)

    scales = []
    for g in range(groups):
        at = 8 * g
        head = [column(g, at + k) for k in range(8)]
        own, pivots, steps = state[g], None, []
        for k in range(0, 8, 2):
            u, v = head[k], head[k + 1]
            a, b, c = u[k:k + 1, :], v[k:k + 1, :], v[k + 1:k + 2, :]
            inverse = 1.0 / (a * c - b * b)
            rest = sub > k + 1
            first = jnp.where(rest, u * c - v * b, 0.0) * inverse
            second = jnp.where(rest, v * a - u * b, 0.0) * inverse
            here, there = lane == at + k, lane == at + k + 1
            lines = own[k:k + 1, :], own[k + 1:k + 2, :]
            rows = (jnp.where(here, 1.0, jnp.where(there, 0.0, lines[0])),
                    jnp.where(here, 0.0, jnp.where(there, 1.0, lines[1])))
            for m in range(k + 2, 8):
                head[m] = head[m] - (first * head[m][k:k + 1, :] + second * head[m][k + 1:k + 2, :])
            own = jnp.where(rest & (here | there), 0.0, own) - (first * rows[0] + second * rows[1])
            ratio = b / a
            own = jnp.where(sub == k + 1, rows[1] - ratio * rows[0], own)
            pivots = a if k == 0 else jnp.where(sub >= k, a, pivots)
            pivots = jnp.where(sub > k, c - b * ratio, pivots)
            later = (lane > at + k + 1) & (lane < at + 8)
            rows = [jnp.where(later, 0.0, row) for row in rows]
            steps.append((k, c * inverse, b * inverse, a * inverse, rows))
        state[g] = own
        scales.append(lax.rsqrt(pivots))
        inside = (lane >= at) & (lane < at + 8)
        for h in range(g + 1, groups):
            below = [column(h, at + k) for k in range(8)]
            value = jnp.where(inside, 0.0, state[h])
            for k, p, q, r, rows in steps:
                u, v = below[k], below[k + 1]
                first, second = u * p - v * q, v * r - u * q
                for m in range(k + 2, 8):
                    below[m] = below[m] - (first * head[m][k:k + 1, :] + second * head[m][k + 1:k + 2, :])
                value = value - (first * rows[0] + second * rows[1])
            state[h] = value
        beside(g)
    result = []
    for g in range(groups):
        value = jnp.where(lane < 8 * g + sub, state[g], jnp.where(lane == 8 * g + sub, 1.0, 0.0))
        result.append(value * scales[g] * along)
    return jnp.concatenate(result, axis=0)


def stack(value):
    return jnp.concatenate(split(value), axis=0)


def times(stacked, parts, dim=0):
    high, mid, low = parts
    n = RANK
    first, second, third = dot(stacked, high, dim), dot(stacked[:2 * n], mid, dim), dot(stacked[:n], low, dim)
    small = first[2 * n:] + second[n:] + third
    return first[:n] + (first[n:2 * n] + second[:n] + small)


def finish_kernel(factor, flat_ref, test_ref, x_hbm, basis_ref, projected_ref, x_ref, c_ref, parts_ref, sem):
    x_copy = pltpu.make_async_copy(x_hbm, x_ref, sem)
    x_copy.start()
    row, col = iota(0), iota(1)

    def place(a, b, value):
        for k, part in enumerate(split(value)):
            c_ref[k, a * BLOCK:(a + 1) * BLOCK, b * BLOCK:(b + 1) * BLOCK] = part

    for n, (a, b) in enumerate(UPPER):
        value = flat_ref[n * BLOCK:(n + 1) * BLOCK, :]
        place(a, b, value)
        place(b, a, value.T)
    for i in range(NB // 2):
        value = flat_ref[PACKED + i * BLOCK:PACKED + (i + 1) * BLOCK, :]
        flipped = value.T
        place(2 * i, 2 * i, jnp.where(row <= col, value, flipped))
        other = jnp.where(row > col, value, flipped)
        place(2 * i + 1, 2 * i + 1, jnp.where(row == col, flat_ref[DIAGS + i:DIAGS + i + 1, :], other))

    def part_rows(start, size):
        at = slice(start, start + size)
        parts_ref[0, at, :], parts_ref[1, at, :] = halves(x_ref[at, :])

    covariance = [c_ref.at[k] for k in range(3)]
    test = stack(test_ref[:RANK, :])
    image = times(test, [part[...] for part in covariance])
    gram = times(test, split(image), 1)
    first = inverse_factor(gram, lambda g: None)
    spanned = times(stack(first), split(image))
    spanned_stack = stack(spanned)
    reach = times(spanned_stack, [part[...] for part in covariance])
    gram = times(spanned_stack, split(reach), 1)
    x_copy.wait()
    step = x_ref.shape[0] // 7
    second = inverse_factor(gram, lambda g: part_rows(step * g, step) if g < 7 else None)
    second_stack = stack(second)
    projected_ref[...] = times(second_stack, split(reach)) * (1.0 / factor)
    weight = jnp.concatenate(halves(times(second_stack, split(spanned)) * factor), axis=0)
    main, rest = dot(weight, parts_ref[0], 1), dot(weight, parts_ref[1], 1)
    basis_ref[...] = main[:RANK] + (main[RANK:] + rest[:RANK] + rest[RANK:])


def tree(parts):
    while len(parts) > 1:
        parts = [parts[i] + parts[i + 1] for i in range(0, len(parts), 2)]
    return parts[0]


def everyone(value, axis, size):
    return lax.all_to_all(jnp.broadcast_to(value, (size,) + value.shape), axis, 0, 0)


def pick(array, i):
    return lax.dynamic_index_in_dim(array, i, 0, keepdims=False)


def stacked_sum(values):
    return tree([values[i] for i in range(values.shape[0])])


def total(flat):
    core = lax.axis_index("core")
    swap = [(0, 1), (1, 0)]
    pair = flat.reshape(2, FLAT // 2, BLOCK)
    value = pick(pair, core) + lax.ppermute(pick(pair, 1 - core), "core", swap)
    value = stacked_sum(lax.all_to_all(value.reshape(SX, -1, BLOCK), "x", 0, 0))
    value = stacked_sum(lax.all_to_all(value.reshape(SY, -1, BLOCK), "y", 0, 0))
    value = stacked_sum(everyone(value, "z", SZ))
    value = everyone(value, "y", SY).reshape(-1, BLOCK)
    value = everyone(value, "x", SX).reshape(-1, BLOCK)
    other = lax.ppermute(value, "core", swap)
    low = jnp.where(core == 0, value, other)
    high = jnp.where(core == 0, other, value)
    return jnp.concatenate([low, high])


def local(embeddings, test_matrix):
    rows = embeddings.shape[0]
    factor = float(np.sqrt(np.float32(rows * 2 * SX * SY * SZ)))
    flat = pl.pallas_call(
        gram_kernel,
        in_specs=[pl.BlockSpec(memory_space=pl.ANY)],
        out_specs=pl.BlockSpec(memory_space=pltpu.VMEM),
        out_shape=jax.ShapeDtypeStruct((FLAT, BLOCK), jnp.float32),
        scratch_shapes=[pltpu.VMEM((rows, D), jnp.float32)]
        + [pltpu.VMEM((CHUNKS[-1][0] + 512, D), jnp.bfloat16)] * 2
        + [pltpu.VMEM((9, 256, 256), jnp.float32)] * 2
        + [pltpu.SemaphoreType.DMA((len(CHUNKS),))],
        compiler_params=pltpu.CompilerParams(vmem_limit_bytes=50 * 2 ** 20),
        cost_estimate=pl.CostEstimate(flops=2 * rows * D * D * 2, bytes_accessed=4 * rows * D, transcendentals=0),
    )(embeddings)
    flat = total(flat)
    basis, projected = pl.pallas_call(
        lambda *refs: finish_kernel(factor, *refs),
        in_specs=[pl.BlockSpec(memory_space=pltpu.VMEM)] * 2 + [pl.BlockSpec(memory_space=pl.ANY)],
        out_specs=[pl.BlockSpec(memory_space=pltpu.VMEM)] * 2,
        out_shape=[jax.ShapeDtypeStruct((RANK, rows), jnp.float32), jax.ShapeDtypeStruct((RANK, D), jnp.float32)],
        scratch_shapes=[
            pltpu.VMEM((rows, D), jnp.float32),
            pltpu.VMEM((3, D, D), jnp.bfloat16),
            pltpu.VMEM((2, rows, D), jnp.bfloat16),
            pltpu.SemaphoreType.DMA,
        ],
        compiler_params=pltpu.CompilerParams(vmem_limit_bytes=50 * 2 ** 20),
        cost_estimate=pl.CostEstimate(flops=2 * rows * D * RANK * 8, bytes_accessed=4 * rows * D, transcendentals=0),
    )(flat, jnp.pad(test_matrix.T, ((0, 8), (0, 0))), embeddings)
    return basis.T, projected


def solution(mesh):
    grid = Mesh(mesh.devices.reshape(SX, SY, SZ, 2), ("x", "y", "z", "core"))
    in_specs = (P(("x", "y", "z", "core"), None), P())
    out_specs = (P(("x", "y", "z", "core"), None), P())
    return jax.shard_map(local, mesh=grid, in_specs=in_specs, out_specs=out_specs, check_vma=False)
```

```python
import jax
import jax.numpy as jnp
import numpy as np
from jax import lax
from jax.experimental import pallas as pl
from jax.experimental.pallas import tpu as pltpu
from jax.sharding import Mesh, PartitionSpec as P

SX, SY, SZ = 4, 8, 8
D, RANK = 768, 80
BLOCK = 128
NB = D // BLOCK
UPPER = [(a, b) for a in range(NB) for b in range(a + 1, NB)]
PACKED = len(UPPER) * BLOCK
DIAGS = PACKED + NB // 2 * BLOCK
FLAT = 2560
CHUNKS = ((0, 256), (256, 512), (768, 576))
LIMIT = 45 * 2 ** 20


def split(value):
    high = value.astype(jnp.bfloat16)
    rest = value - high.astype(jnp.float32)
    mid = rest.astype(jnp.bfloat16)
    low = (rest - mid.astype(jnp.float32)).astype(jnp.bfloat16)
    return high, mid, low


def halves(value):
    high = value.astype(jnp.bfloat16)
    return high, (value - high.astype(jnp.float32)).astype(jnp.bfloat16)


def dot(left, right, dim=0):
    return lax.dot_general(left, right, (((1,), (dim,)), ((), ())), preferred_element_type=jnp.float32)


def iota(axis):
    return lax.broadcasted_iota(jnp.int32, (BLOCK, BLOCK), axis)


def gram_kernel(x_hbm, flat_ref, high_ref, mid_ref, x_ref, even_ref, odd_ref, sem):
    copies = []
    for n, (start, size) in enumerate(CHUNKS):
        at = pl.ds(start, size)
        copies.append(pltpu.make_async_copy(x_hbm.at[at, :], x_ref.at[at, :], sem.at[n]))
        copies[-1].start()
    used = x_ref.shape[0]
    for ref in (high_ref, mid_ref):
        ref[used:, :] = jnp.zeros((ref.shape[0] - used, D), jnp.bfloat16)

    def arrive(n):
        start, size = CHUNKS[n]
        copies[n].wait()
        at = slice(start, start + size)
        high_ref[at, :], mid_ref[at, :] = halves(x_ref[at, :])

    arrive(0)
    for n, (start, size) in enumerate(CHUNKS):
        deep = slice(start, start + (size + 127) // 128 * 128)
        for i in range(3):
            high_t = high_ref[deep, 256 * i:256 * (i + 1)].T
            for j in range(3):
                cols = slice(256 * j, 256 * (j + 1))
                if i <= j:
                    value = dot(high_t, high_ref[deep, cols])
                    even_ref[3 * i + j] = value if n == 0 else even_ref[3 * i + j] + value
                value = dot(high_t, mid_ref[deep, cols])
                odd_ref[3 * i + j] = value if n == 0 else odd_ref[3 * i + j] + value
            if i == 0 and n + 1 < len(CHUNKS):
                arrive(n + 1)

    row, col = iota(0), iota(1)
    flat_ref[DIAGS:, :] = jnp.zeros((FLAT - DIAGS, BLOCK), jnp.float32)
    for i in range(3):
        for j in range(i, 3):
            value = even_ref[3 * i + j] + (odd_ref[3 * i + j] + odd_ref[3 * j + i].T)
            for p in range(2):
                for q in range(2):
                    a, b = 2 * i + p, 2 * j + q
                    if a < b:
                        at = UPPER.index((a, b)) * BLOCK
                        flat_ref[at:at + BLOCK, :] = value[p * BLOCK:(p + 1) * BLOCK, q * BLOCK:(q + 1) * BLOCK]
            if i == j:
                first, second = value[:BLOCK, :BLOCK], value[BLOCK:, BLOCK:]
                at = PACKED + i * BLOCK
                flat_ref[at:at + BLOCK, :] = jnp.where(row <= col, first, second)
                flat_ref[DIAGS + i:DIAGS + i + 1, :] = jnp.sum(jnp.where(row == col, second, 0.0), axis=0, keepdims=True)


def inverse_factor(gram):
    groups, shape = RANK // 8, (8, RANK)
    lane = lax.broadcasted_iota(jnp.int32, shape, 1)
    sub = lax.broadcasted_iota(jnp.int32, shape, 0)
    state = [gram[8 * g:8 * g + 8, :] for g in range(groups)]
    diagonal = [jnp.where(lane == 8 * g + sub, state[g], 0.0) for g in range(groups)]
    along = lax.rsqrt(jnp.sum(sum(diagonal[1:], diagonal[0]), axis=0, keepdims=True))
    state = [state[g] * lax.rsqrt(jnp.sum(diagonal[g], axis=1, keepdims=True)) * along for g in range(groups)]

    def column(h, j):
        return jnp.broadcast_to(state[h][:, j:j + 1], shape)

    def line(value, i):
        return jnp.broadcast_to(value[i:i + 1, :], shape)

    scales = []
    coming = [column(0, k) for k in range(8)]
    for g in range(groups):
        at = 8 * g
        head = coming
        own, pivots, steps = state[g], None, []
        for k in range(0, 8, 2):
            u, v = head[k], head[k + 1]
            a, b, c = line(u, k), line(v, k), line(v, k + 1)
            inverse = 1.0 / (a * c - b * b)
            rest = sub > k + 1
            first = jnp.where(rest, u * c - v * b, 0.0) * inverse
            second = jnp.where(rest, v * a - u * b, 0.0) * inverse
            here, there = lane == at + k, lane == at + k + 1
            rows = (jnp.where(here, 1.0, jnp.where(there, 0.0, line(own, k))),
                    jnp.where(here, 0.0, jnp.where(there, 1.0, line(own, k + 1))))
            pairs = {m: (line(head[m], k), line(head[m], k + 1)) for m in range(k + 2, 8)}
            for m in range(k + 2, 8):
                head[m] = head[m] - (first * pairs[m][0] + second * pairs[m][1])
            own = jnp.where(rest & (here | there), 0.0, own) - (first * rows[0] + second * rows[1])
            ratio = b / a
            own = jnp.where(sub == k + 1, rows[1] - ratio * rows[0], own)
            pivots = a if k == 0 else jnp.where(sub >= k, a, pivots)
            pivots = jnp.where(sub > k, c - b * ratio, pivots)
            later = (lane > at + k + 1) & (lane < at + 8)
            rows = [jnp.where(later, 0.0, row) for row in rows]
            steps.append((k, c * inverse, b * inverse, a * inverse, rows, pairs))
        state[g] = own
        scales.append(lax.rsqrt(pivots))
        inside = (lane >= at) & (lane < at + 8)
        for h in range(g + 1, groups):
            below = [column(h, at + k) for k in range(8)]
            value = jnp.where(inside, 0.0, state[h])
            if h == g + 1:
                coming = [column(h, at + 8 + k) for k in range(8)]
            for k, p, q, r, rows, pairs in steps:
                u, v = below[k], below[k + 1]
                first, second = u * p - v * q, v * r - u * q
                if h == g + 1:
                    coming = [coming[m] - (first * line(u, m) + second * line(v, m)) for m in range(8)]
                for m in range(k + 2, 8):
                    below[m] = below[m] - (first * pairs[m][0] + second * pairs[m][1])
                value = value - (first * rows[0] + second * rows[1])
            state[h] = value
    result = []
    for g in range(groups):
        value = jnp.where(lane < 8 * g + sub, state[g], jnp.where(lane == 8 * g + sub, 1.0, 0.0))
        result.append(value * scales[g] * along)
    return jnp.concatenate(result, axis=0)


def stack(value):
    return jnp.concatenate(split(value), axis=0)


def times(stacked, parts, dim=0):
    high, mid, low = parts
    n = RANK
    first, second, third = dot(stacked, high, dim), dot(stacked[:2 * n], mid, dim), dot(stacked[:n], low, dim)
    small = first[2 * n:] + second[n:] + third
    return first[:n] + (first[n:2 * n] + second[:n] + small)


def finish_kernel(factor, flat_ref, test_ref, high_ref, mid_ref, basis_ref, projected_ref, c_ref):
    row, col = iota(0), iota(1)

    def place(a, b, value):
        for k, part in enumerate(split(value)):
            c_ref[k, a * BLOCK:(a + 1) * BLOCK, b * BLOCK:(b + 1) * BLOCK] = part

    test = stack(test_ref[:RANK, :])
    image = None
    for i in range(NB // 2):
        for n, (a, b) in enumerate(UPPER):
            if a // 2 == i:
                value = flat_ref[n * BLOCK:(n + 1) * BLOCK, :]
                place(a, b, value)
                place(b, a, value.T)
        value = flat_ref[PACKED + i * BLOCK:PACKED + (i + 1) * BLOCK, :]
        flipped = value.T
        place(2 * i, 2 * i, jnp.where(row <= col, value, flipped))
        other = jnp.where(row > col, value, flipped)
        place(2 * i + 1, 2 * i + 1, jnp.where(row == col, flat_ref[DIAGS + i:DIAGS + i + 1, :], other))
        deep = slice(256 * i, 256 * (i + 1))
        value = times(test[:, deep], [c_ref[k, deep, :] for k in range(3)])
        image = value if i == 0 else image + value

    covariance = [c_ref.at[k] for k in range(3)]
    gram = times(test, split(image), 1)
    first = inverse_factor(gram)
    spanned = times(stack(first), split(image))
    spanned_stack = stack(spanned)
    reach = times(spanned_stack, [part[...] for part in covariance])
    gram = times(spanned_stack, split(reach), 1)
    second = inverse_factor(gram)
    second_stack = stack(second)
    projected_ref[...] = times(second_stack, split(reach)) * (1.0 / factor)
    empty = jnp.zeros((BLOCK - RANK, D), jnp.float32)
    weight = jnp.concatenate([times(second_stack, split(spanned)) * factor, empty], axis=0)
    weight = jnp.concatenate(halves(weight), axis=0).T
    total_rows = basis_ref.shape[1]
    for start in range(0, total_rows, 256):
        size = min(256, total_rows - start)
        at = slice(start, start + size)
        main, rest = dot(high_ref[at, :], weight), dot(mid_ref[at, :], weight)
        value = main[:, :BLOCK] + (main[:, BLOCK:] + (rest[:, :BLOCK] + rest[:, BLOCK:]))
        basis_ref[:, at] = value.T[:RANK, :]


def tree(parts):
    while len(parts) > 1:
        parts = [parts[i] + parts[i + 1] for i in range(0, len(parts), 2)]
    return parts[0]


def everyone(value, axis, size):
    return lax.all_to_all(jnp.broadcast_to(value, (size,) + value.shape), axis, 0, 0)


def pick(array, i):
    return lax.dynamic_index_in_dim(array, i, 0, keepdims=False)


def stacked_sum(values):
    return tree([values[i] for i in range(values.shape[0])])


def total(flat):
    core = lax.axis_index("core")
    swap = [(0, 1), (1, 0)]
    pair = flat.reshape(2, FLAT // 2, BLOCK)
    value = pick(pair, core) + lax.ppermute(pick(pair, 1 - core), "core", swap)
    value = stacked_sum(lax.all_to_all(value.reshape(SX, -1, BLOCK), "x", 0, 0))
    value = stacked_sum(lax.all_to_all(value.reshape(SY, -1, BLOCK), "y", 0, 0))
    value = stacked_sum(everyone(value, "z", SZ))
    value = everyone(value, "y", SY).reshape(-1, BLOCK)
    value = everyone(value, "x", SX).reshape(-1, BLOCK)
    other = lax.ppermute(value, "core", swap)
    low = jnp.where(core == 0, value, other)
    high = jnp.where(core == 0, other, value)
    return jnp.concatenate([low, high])


def local(embeddings, test_matrix):
    rows = embeddings.shape[0]
    factor = float(np.sqrt(np.float32(rows * 2 * SX * SY * SZ)))
    held = CHUNKS[-1][0] + (CHUNKS[-1][1] + 127) // 128 * 128
    flat, high, mid = pl.pallas_call(
        gram_kernel,
        in_specs=[pl.BlockSpec(memory_space=pl.ANY)],
        out_specs=[pl.BlockSpec(memory_space=pltpu.VMEM)] * 3,
        out_shape=[jax.ShapeDtypeStruct((FLAT, BLOCK), jnp.float32)] + [jax.ShapeDtypeStruct((held, D), jnp.bfloat16)] * 2,
        scratch_shapes=[pltpu.VMEM((rows, D), jnp.float32)]
        + [pltpu.VMEM((9, 256, 256), jnp.float32)] * 2
        + [pltpu.SemaphoreType.DMA((len(CHUNKS),))],
        compiler_params=pltpu.CompilerParams(vmem_limit_bytes=LIMIT),
        cost_estimate=pl.CostEstimate(flops=2 * rows * D * D * 2, bytes_accessed=4 * rows * D, transcendentals=0),
    )(embeddings)
    flat = total(flat)
    basis, projected = pl.pallas_call(
        lambda *refs: finish_kernel(factor, *refs),
        in_specs=[pl.BlockSpec(memory_space=pltpu.VMEM)] * 4,
        out_specs=[pl.BlockSpec(memory_space=pltpu.VMEM)] * 2,
        out_shape=[jax.ShapeDtypeStruct((RANK, rows), jnp.float32), jax.ShapeDtypeStruct((RANK, D), jnp.float32)],
        scratch_shapes=[pltpu.VMEM((3, D, D), jnp.bfloat16)],
        compiler_params=pltpu.CompilerParams(vmem_limit_bytes=LIMIT),
        cost_estimate=pl.CostEstimate(flops=2 * rows * D * RANK * 8, bytes_accessed=4 * rows * D, transcendentals=0),
    )(flat, jnp.pad(test_matrix.T, ((0, 8), (0, 0))), high, mid)
    return basis.T, projected


def solution(mesh):
    grid = Mesh(mesh.devices.reshape(SX, SY, SZ, 2), ("x", "y", "z", "core"))
    in_specs = (P(("x", "y", "z", "core"), None), P())
    out_specs = (P(("x", "y", "z", "core"), None), P())
    return jax.shard_map(local, mesh=grid, in_specs=in_specs, out_specs=out_specs, check_vma=False)
```

```python
import jax
import jax.numpy as jnp
import numpy as np
from jax import lax
from jax.experimental import pallas as pl
from jax.experimental.pallas import tpu as pltpu
from jax.sharding import Mesh, PartitionSpec as P

SX, SY, SZ = 4, 8, 8
D, RANK = 768, 80
BLOCK = 128
NB = D // BLOCK
UPPER = [(a, b) for a in range(NB) for b in range(a + 1, NB)]
PACKED = len(UPPER) * BLOCK
DIAGS = PACKED + NB // 2 * BLOCK
FLAT = 2560
CHUNKS = ((0, 256), (256, 512), (768, 576))
LIMIT = 50 * 2 ** 20


def split(value):
    high = value.astype(jnp.bfloat16)
    rest = value - high.astype(jnp.float32)
    mid = rest.astype(jnp.bfloat16)
    low = (rest - mid.astype(jnp.float32)).astype(jnp.bfloat16)
    return high, mid, low


def halves(value):
    high = value.astype(jnp.bfloat16)
    return high, (value - high.astype(jnp.float32)).astype(jnp.bfloat16)


def dot(left, right, dim=0):
    return lax.dot_general(left, right, (((1,), (dim,)), ((), ())), preferred_element_type=jnp.float32)


def iota(axis):
    return lax.broadcasted_iota(jnp.int32, (BLOCK, BLOCK), axis)


def gram_kernel(x_hbm, flat_ref, high_hbm, mid_hbm, x_ref, high_ref, mid_ref, even_ref, odd_ref, sem, out_sem):
    copies = []
    for n, (start, size) in enumerate(CHUNKS):
        at = pl.ds(start, size)
        copies.append(pltpu.make_async_copy(x_hbm.at[at, :], x_ref.at[at, :], sem.at[n]))
        copies[-1].start()
    used = x_ref.shape[0]
    for ref in (high_ref, mid_ref):
        ref[used:, :] = jnp.zeros((ref.shape[0] - used, D), jnp.bfloat16)

    def arrive(n):
        start, size = CHUNKS[n]
        copies[n].wait()
        at = slice(start, start + size)
        high_ref[at, :], mid_ref[at, :] = halves(x_ref[at, :])
        for k, (part, hbm) in enumerate(((high_ref, high_hbm), (mid_ref, mid_hbm))):
            keeps.append(pltpu.make_async_copy(part.at[at, :], hbm.at[at, :], out_sem.at[n, k]))
            keeps[-1].start()

    keeps = []
    arrive(0)
    for n, (start, size) in enumerate(CHUNKS):
        deep = slice(start, start + (size + 127) // 128 * 128)
        for i in range(3):
            high_t = high_ref[deep, 256 * i:256 * (i + 1)].T
            for j in range(3):
                cols = slice(256 * j, 256 * (j + 1))
                if i <= j:
                    value = dot(high_t, high_ref[deep, cols])
                    even_ref[3 * i + j] = value if n == 0 else even_ref[3 * i + j] + value
                value = dot(high_t, mid_ref[deep, cols])
                odd_ref[3 * i + j] = value if n == 0 else odd_ref[3 * i + j] + value
            if i == 0 and n + 1 < len(CHUNKS):
                arrive(n + 1)

    row, col = iota(0), iota(1)
    flat_ref[DIAGS:, :] = jnp.zeros((FLAT - DIAGS, BLOCK), jnp.float32)
    for i in range(3):
        for j in range(i, 3):
            value = even_ref[3 * i + j] + (odd_ref[3 * i + j] + odd_ref[3 * j + i].T)
            for p in range(2):
                for q in range(2):
                    a, b = 2 * i + p, 2 * j + q
                    if a < b:
                        at = UPPER.index((a, b)) * BLOCK
                        flat_ref[at:at + BLOCK, :] = value[p * BLOCK:(p + 1) * BLOCK, q * BLOCK:(q + 1) * BLOCK]
            if i == j:
                first, second = value[:BLOCK, :BLOCK], value[BLOCK:, BLOCK:]
                at = PACKED + i * BLOCK
                flat_ref[at:at + BLOCK, :] = jnp.where(row <= col, first, second)
                flat_ref[DIAGS + i:DIAGS + i + 1, :] = jnp.sum(jnp.where(row == col, second, 0.0), axis=0, keepdims=True)
    for copy in keeps:
        copy.wait()


def inverse_factor(gram):
    groups, shape = RANK // 8, (8, RANK)
    lane = lax.broadcasted_iota(jnp.int32, shape, 1)
    sub = lax.broadcasted_iota(jnp.int32, shape, 0)
    state = [gram[8 * g:8 * g + 8, :] for g in range(groups)]
    diagonal = [jnp.where(lane == 8 * g + sub, state[g], 0.0) for g in range(groups)]
    along = lax.rsqrt(jnp.sum(sum(diagonal[1:], diagonal[0]), axis=0, keepdims=True))
    state = [state[g] * lax.rsqrt(jnp.sum(diagonal[g], axis=1, keepdims=True)) * along for g in range(groups)]

    def column(h, j):
        return jnp.broadcast_to(state[h][:, j:j + 1], shape)

    def line(value, i):
        return jnp.broadcast_to(value[i:i + 1, :], shape)

    scales = []
    coming = [column(0, k) for k in range(8)]
    for g in range(groups):
        at = 8 * g
        head = coming
        own, pivots, steps = state[g], None, []
        for k in range(0, 8, 2):
            u, v = head[k], head[k + 1]
            a, b, c = line(u, k), line(v, k), line(v, k + 1)
            inverse = 1.0 / (a * c - b * b)
            rest = sub > k + 1
            first = jnp.where(rest, u * c - v * b, 0.0) * inverse
            second = jnp.where(rest, v * a - u * b, 0.0) * inverse
            here, there = lane == at + k, lane == at + k + 1
            rows = (jnp.where(here, 1.0, jnp.where(there, 0.0, line(own, k))),
                    jnp.where(here, 0.0, jnp.where(there, 1.0, line(own, k + 1))))
            pairs = {m: (line(head[m], k), line(head[m], k + 1)) for m in range(k + 2, 8)}
            for m in range(k + 2, 8):
                head[m] = head[m] - (first * pairs[m][0] + second * pairs[m][1])
            own = jnp.where(rest & (here | there), 0.0, own) - (first * rows[0] + second * rows[1])
            ratio = b / a
            own = jnp.where(sub == k + 1, rows[1] - ratio * rows[0], own)
            pivots = a if k == 0 else jnp.where(sub >= k, a, pivots)
            pivots = jnp.where(sub > k, c - b * ratio, pivots)
            later = (lane > at + k + 1) & (lane < at + 8)
            rows = [jnp.where(later, 0.0, row) for row in rows]
            steps.append((k, c * inverse, b * inverse, a * inverse, rows, pairs))
        state[g] = own
        scales.append(lax.rsqrt(pivots))
        inside = (lane >= at) & (lane < at + 8)
        for h in range(g + 1, groups):
            below = [column(h, at + k) for k in range(8)]
            value = jnp.where(inside, 0.0, state[h])
            if h == g + 1:
                coming = [column(h, at + 8 + k) for k in range(8)]
            for k, p, q, r, rows, pairs in steps:
                u, v = below[k], below[k + 1]
                first, second = u * p - v * q, v * r - u * q
                if h == g + 1:
                    coming = [coming[m] - (first * line(u, m) + second * line(v, m)) for m in range(8)]
                for m in range(k + 2, 8):
                    below[m] = below[m] - (first * pairs[m][0] + second * pairs[m][1])
                value = value - (first * rows[0] + second * rows[1])
            state[h] = value
    result = []
    for g in range(groups):
        value = jnp.where(lane < 8 * g + sub, state[g], jnp.where(lane == 8 * g + sub, 1.0, 0.0))
        result.append(value * scales[g] * along)
    return jnp.concatenate(result, axis=0)


def stack(value):
    return jnp.concatenate(split(value), axis=0)


def times(stacked, parts, dim=0):
    high, mid, low = parts
    n = RANK
    first, second, third = dot(stacked, high, dim), dot(stacked[:2 * n], mid, dim), dot(stacked[:n], low, dim)
    small = first[2 * n:] + second[n:] + third
    return first[:n] + (first[n:2 * n] + second[:n] + small)


def finish_kernel(factor, flat_ref, test_ref, high_hbm, mid_hbm, basis_ref, projected_ref, high_ref, mid_ref, c_ref, sem):
    copies = [pltpu.make_async_copy(hbm, ref, sem.at[k])
              for k, (hbm, ref) in enumerate(((high_hbm, high_ref), (mid_hbm, mid_ref)))]
    for copy in copies:
        copy.start()
    row, col = iota(0), iota(1)

    def place(a, b, value):
        for k, part in enumerate(split(value)):
            c_ref[k, a * BLOCK:(a + 1) * BLOCK, b * BLOCK:(b + 1) * BLOCK] = part

    test = stack(test_ref[:RANK, :])
    image = None
    for i in range(NB // 2):
        for n, (a, b) in enumerate(UPPER):
            if a // 2 == i:
                value = flat_ref[n * BLOCK:(n + 1) * BLOCK, :]
                place(a, b, value)
                place(b, a, value.T)
        value = flat_ref[PACKED + i * BLOCK:PACKED + (i + 1) * BLOCK, :]
        flipped = value.T
        place(2 * i, 2 * i, jnp.where(row <= col, value, flipped))
        other = jnp.where(row > col, value, flipped)
        place(2 * i + 1, 2 * i + 1, jnp.where(row == col, flat_ref[DIAGS + i:DIAGS + i + 1, :], other))
        deep = slice(256 * i, 256 * (i + 1))
        value = times(test[:, deep], [c_ref[k, deep, :] for k in range(3)])
        image = value if i == 0 else image + value

    covariance = [c_ref.at[k] for k in range(3)]
    gram = times(test, split(image), 1)
    first = inverse_factor(gram)
    spanned = times(stack(first), split(image))
    spanned_stack = stack(spanned)
    reach = times(spanned_stack, [part[...] for part in covariance])
    gram = times(spanned_stack, split(reach), 1)
    second = inverse_factor(gram)
    second_stack = stack(second)
    projected_ref[...] = times(second_stack, split(reach)) * (1.0 / factor)
    for copy in copies:
        copy.wait()
    empty = jnp.zeros((BLOCK - RANK, D), jnp.float32)
    weight = jnp.concatenate([times(second_stack, split(spanned)) * factor, empty], axis=0)
    weight = jnp.concatenate(halves(weight), axis=0).T
    total_rows = basis_ref.shape[1]
    for start in range(0, total_rows, 256):
        size = min(256, total_rows - start)
        at = slice(start, start + size)
        main, rest = dot(high_ref[at, :], weight), dot(mid_ref[at, :], weight)
        value = main[:, :BLOCK] + (main[:, BLOCK:] + (rest[:, :BLOCK] + rest[:, BLOCK:]))
        basis_ref[:, at] = value.T[:RANK, :]


def tree(parts):
    while len(parts) > 1:
        parts = [parts[i] + parts[i + 1] for i in range(0, len(parts), 2)]
    return parts[0]


def everyone(value, axis, size):
    return lax.all_to_all(jnp.broadcast_to(value, (size,) + value.shape), axis, 0, 0)


def pick(array, i):
    return lax.dynamic_index_in_dim(array, i, 0, keepdims=False)


def stacked_sum(values):
    return tree([values[i] for i in range(values.shape[0])])


def total(flat):
    core = lax.axis_index("core")
    swap = [(0, 1), (1, 0)]
    pair = flat.reshape(2, FLAT // 2, BLOCK)
    value = pick(pair, core) + lax.ppermute(pick(pair, 1 - core), "core", swap)
    value = stacked_sum(lax.all_to_all(value.reshape(SX, -1, BLOCK), "x", 0, 0))
    value = stacked_sum(lax.all_to_all(value.reshape(SY, -1, BLOCK), "y", 0, 0))
    value = stacked_sum(everyone(value, "z", SZ))
    value = everyone(value, "y", SY).reshape(-1, BLOCK)
    value = everyone(value, "x", SX).reshape(-1, BLOCK)
    other = lax.ppermute(value, "core", swap)
    low = jnp.where(core == 0, value, other)
    high = jnp.where(core == 0, other, value)
    return jnp.concatenate([low, high])


def local(embeddings, test_matrix):
    rows = embeddings.shape[0]
    factor = float(np.sqrt(np.float32(rows * 2 * SX * SY * SZ)))
    held = CHUNKS[-1][0] + (CHUNKS[-1][1] + 127) // 128 * 128
    flat, high, mid = pl.pallas_call(
        gram_kernel,
        in_specs=[pl.BlockSpec(memory_space=pl.ANY)],
        out_specs=[pl.BlockSpec(memory_space=pltpu.VMEM)] + [pl.BlockSpec(memory_space=pl.ANY)] * 2,
        out_shape=[jax.ShapeDtypeStruct((FLAT, BLOCK), jnp.float32)] + [jax.ShapeDtypeStruct((rows, D), jnp.bfloat16)] * 2,
        scratch_shapes=[pltpu.VMEM((rows, D), jnp.float32)]
        + [pltpu.VMEM((held, D), jnp.bfloat16)] * 2
        + [pltpu.VMEM((9, 256, 256), jnp.float32)] * 2
        + [pltpu.SemaphoreType.DMA((len(CHUNKS),)), pltpu.SemaphoreType.DMA((len(CHUNKS), 2))],
        compiler_params=pltpu.CompilerParams(vmem_limit_bytes=LIMIT),
        cost_estimate=pl.CostEstimate(flops=2 * rows * D * D * 2, bytes_accessed=4 * rows * D, transcendentals=0),
    )(embeddings)
    flat = total(flat)
    basis, projected = pl.pallas_call(
        lambda *refs: finish_kernel(factor, *refs),
        in_specs=[pl.BlockSpec(memory_space=pltpu.VMEM)] * 2 + [pl.BlockSpec(memory_space=pl.ANY)] * 2,
        out_specs=[pl.BlockSpec(memory_space=pltpu.VMEM)] * 2,
        out_shape=[jax.ShapeDtypeStruct((RANK, rows), jnp.float32), jax.ShapeDtypeStruct((RANK, D), jnp.float32)],
        scratch_shapes=[pltpu.VMEM((rows, D), jnp.bfloat16)] * 2
        + [pltpu.VMEM((3, D, D), jnp.bfloat16), pltpu.SemaphoreType.DMA((2,))],
        compiler_params=pltpu.CompilerParams(vmem_limit_bytes=LIMIT),
        cost_estimate=pl.CostEstimate(flops=2 * rows * D * RANK * 8, bytes_accessed=4 * rows * D, transcendentals=0),
    )(flat, jnp.pad(test_matrix.T, ((0, 8), (0, 0))), high, mid)
    return basis.T, projected


def solution(mesh):
    grid = Mesh(mesh.devices.reshape(SX, SY, SZ, 2), ("x", "y", "z", "core"))
    in_specs = (P(("x", "y", "z", "core"), None), P())
    out_specs = (P(("x", "y", "z", "core"), None), P())
    return jax.shard_map(local, mesh=grid, in_specs=in_specs, out_specs=out_specs, check_vma=False)
```

```python
import jax
import jax.numpy as jnp
import numpy as np
from jax import lax
from jax.experimental import pallas as pl
from jax.experimental.pallas import tpu as pltpu
from jax.sharding import Mesh, PartitionSpec as P

SX, SY, SZ = 4, 8, 8
D, RANK = 768, 80
BLOCK = 128
NB = D // BLOCK
UPPER = [(a, b) for a in range(NB) for b in range(a + 1, NB)]
PACKED = len(UPPER) * BLOCK
DIAGS = PACKED + NB // 2 * BLOCK
FLAT = 2560
CHUNKS = ((0, 256), (256, 512), (768, 576))
LIMITS = 45 * 2 ** 20, 45 * 2 ** 20


def split(value):
    high = value.astype(jnp.bfloat16)
    rest = value - high.astype(jnp.float32)
    mid = rest.astype(jnp.bfloat16)
    low = (rest - mid.astype(jnp.float32)).astype(jnp.bfloat16)
    return high, mid, low


def halves(value):
    high = value.astype(jnp.bfloat16)
    return high, (value - high.astype(jnp.float32)).astype(jnp.bfloat16)


def dot(left, right, dim=0):
    return lax.dot_general(left, right, (((1,), (dim,)), ((), ())), preferred_element_type=jnp.float32)


def iota(axis):
    return lax.broadcasted_iota(jnp.int32, (BLOCK, BLOCK), axis)


def gram_kernel(x_hbm, flat_ref, high_ref, mid_ref, x_ref, even_ref, odd_ref, sem):
    copies = []
    for n, (start, size) in enumerate(CHUNKS):
        at = pl.ds(start, size)
        copies.append(pltpu.make_async_copy(x_hbm.at[at, :], x_ref.at[at, :], sem.at[n]))
        copies[-1].start()
    used = x_ref.shape[0]
    for ref in (high_ref, mid_ref):
        ref[used:, :] = jnp.zeros((ref.shape[0] - used, D), jnp.bfloat16)

    def arrive(n):
        start, size = CHUNKS[n]
        copies[n].wait()
        at = slice(start, start + size)
        high_ref[at, :], mid_ref[at, :] = halves(x_ref[at, :])

    arrive(0)
    for n, (start, size) in enumerate(CHUNKS):
        deep = slice(start, start + (size + 127) // 128 * 128)
        for i in range(3):
            high_t = high_ref[deep, 256 * i:256 * (i + 1)].T
            for j in range(3):
                cols = slice(256 * j, 256 * (j + 1))
                if i <= j:
                    value = dot(high_t, high_ref[deep, cols])
                    even_ref[3 * i + j] = value if n == 0 else even_ref[3 * i + j] + value
                value = dot(high_t, mid_ref[deep, cols])
                odd_ref[3 * i + j] = value if n == 0 else odd_ref[3 * i + j] + value
            if i == 0 and n + 1 < len(CHUNKS):
                arrive(n + 1)

    row, col = iota(0), iota(1)
    flat_ref[DIAGS:, :] = jnp.zeros((FLAT - DIAGS, BLOCK), jnp.float32)
    for i in range(3):
        for j in range(i, 3):
            value = even_ref[3 * i + j] + (odd_ref[3 * i + j] + odd_ref[3 * j + i].T)
            for p in range(2):
                for q in range(2):
                    a, b = 2 * i + p, 2 * j + q
                    if a < b:
                        at = UPPER.index((a, b)) * BLOCK
                        flat_ref[at:at + BLOCK, :] = value[p * BLOCK:(p + 1) * BLOCK, q * BLOCK:(q + 1) * BLOCK]
            if i == j:
                first, second = value[:BLOCK, :BLOCK], value[BLOCK:, BLOCK:]
                at = PACKED + i * BLOCK
                flat_ref[at:at + BLOCK, :] = jnp.where(row <= col, first, second)
                flat_ref[DIAGS + i:DIAGS + i + 1, :] = jnp.sum(jnp.where(row == col, second, 0.0), axis=0, keepdims=True)


def inverse_factor(gram):
    groups, shape = RANK // 8, (8, RANK)
    lane = lax.broadcasted_iota(jnp.int32, shape, 1)
    sub = lax.broadcasted_iota(jnp.int32, shape, 0)
    state = [gram[8 * g:8 * g + 8, :] for g in range(groups)]
    diagonal = [jnp.where(lane == 8 * g + sub, state[g], 0.0) for g in range(groups)]
    along = lax.rsqrt(jnp.sum(sum(diagonal[1:], diagonal[0]), axis=0, keepdims=True))
    state = [state[g] * lax.rsqrt(jnp.sum(diagonal[g], axis=1, keepdims=True)) * along for g in range(groups)]

    def column(h, j):
        return jnp.broadcast_to(state[h][:, j:j + 1], shape)

    def line(value, i):
        return jnp.broadcast_to(value[i:i + 1, :], shape)

    scales = []
    coming = [column(0, k) for k in range(8)]
    for g in range(groups):
        at = 8 * g
        head = coming
        own, pivots, steps = state[g], None, []
        for k in range(0, 8, 2):
            u, v = head[k], head[k + 1]
            a, b, c = line(u, k), line(v, k), line(v, k + 1)
            inverse = 1.0 / (a * c - b * b)
            rest = sub > k + 1
            first = jnp.where(rest, u * c - v * b, 0.0) * inverse
            second = jnp.where(rest, v * a - u * b, 0.0) * inverse
            here, there = lane == at + k, lane == at + k + 1
            rows = (jnp.where(here, 1.0, jnp.where(there, 0.0, line(own, k))),
                    jnp.where(here, 0.0, jnp.where(there, 1.0, line(own, k + 1))))
            pairs = {m: (line(head[m], k), line(head[m], k + 1)) for m in range(k + 2, 8)}
            for m in range(k + 2, 8):
                head[m] = head[m] - (first * pairs[m][0] + second * pairs[m][1])
            own = jnp.where(rest & (here | there), 0.0, own) - (first * rows[0] + second * rows[1])
            ratio = b / a
            own = jnp.where(sub == k + 1, rows[1] - ratio * rows[0], own)
            pivots = a if k == 0 else jnp.where(sub >= k, a, pivots)
            pivots = jnp.where(sub > k, c - b * ratio, pivots)
            later = (lane > at + k + 1) & (lane < at + 8)
            rows = [jnp.where(later, 0.0, row) for row in rows]
            steps.append((k, c * inverse, b * inverse, a * inverse, rows, pairs))
        state[g] = own
        scales.append(lax.rsqrt(pivots))
        inside = (lane >= at) & (lane < at + 8)
        for h in range(g + 1, groups):
            below = [column(h, at + k) for k in range(8)]
            value = jnp.where(inside, 0.0, state[h])
            if h == g + 1:
                coming = [column(h, at + 8 + k) for k in range(8)]
            for k, p, q, r, rows, pairs in steps:
                u, v = below[k], below[k + 1]
                first, second = u * p - v * q, v * r - u * q
                if h == g + 1:
                    coming = [coming[m] - (first * line(u, m) + second * line(v, m)) for m in range(8)]
                for m in range(k + 2, 8):
                    below[m] = below[m] - (first * pairs[m][0] + second * pairs[m][1])
                value = value - (first * rows[0] + second * rows[1])
            state[h] = value
    result = []
    for g in range(groups):
        value = jnp.where(lane < 8 * g + sub, state[g], jnp.where(lane == 8 * g + sub, 1.0, 0.0))
        result.append(value * scales[g] * along)
    return jnp.concatenate(result, axis=0)


def stack(value):
    return jnp.concatenate(split(value), axis=0)


def times(stacked, parts, dim=0):
    high, mid, low = parts
    n = RANK
    first, second, third = dot(stacked, high, dim), dot(stacked[:2 * n], mid, dim), dot(stacked[:n], low, dim)
    small = first[2 * n:] + second[n:] + third
    return first[:n] + (first[n:2 * n] + second[:n] + small)


def finish_kernel(factor, flat_ref, test_ref, high_ref, mid_ref, basis_ref, projected_ref, c_ref):
    row, col = iota(0), iota(1)

    def place(a, b, value):
        for k, part in enumerate(split(value)):
            c_ref[k, a * BLOCK:(a + 1) * BLOCK, b * BLOCK:(b + 1) * BLOCK] = part

    test = stack(test_ref[:RANK, :])
    image = None
    for i in range(NB // 2):
        for n, (a, b) in enumerate(UPPER):
            if a // 2 == i:
                value = flat_ref[n * BLOCK:(n + 1) * BLOCK, :]
                place(a, b, value)
                place(b, a, value.T)
        value = flat_ref[PACKED + i * BLOCK:PACKED + (i + 1) * BLOCK, :]
        flipped = value.T
        place(2 * i, 2 * i, jnp.where(row <= col, value, flipped))
        other = jnp.where(row > col, value, flipped)
        place(2 * i + 1, 2 * i + 1, jnp.where(row == col, flat_ref[DIAGS + i:DIAGS + i + 1, :], other))
        deep = slice(256 * i, 256 * (i + 1))
        value = times(test[:, deep], [c_ref[k, deep, :] for k in range(3)])
        image = value if i == 0 else image + value

    covariance = [c_ref.at[k] for k in range(3)]
    gram = times(test, split(image), 1)
    first = inverse_factor(gram)
    spanned = times(stack(first), split(image))
    spanned_stack = stack(spanned)
    reach = times(spanned_stack, [part[...] for part in covariance])
    gram = times(spanned_stack, split(reach), 1)
    second = inverse_factor(gram)
    second_stack = stack(second)
    projected_ref[...] = times(second_stack, split(reach)) * (1.0 / factor)
    empty = jnp.zeros((BLOCK - RANK, D), jnp.float32)
    weight = jnp.concatenate([times(second_stack, split(spanned)) * factor, empty], axis=0)
    weight = jnp.concatenate(halves(weight), axis=0).T
    total_rows = basis_ref.shape[1]
    for start in range(0, total_rows, 256):
        size = min(256, total_rows - start)
        at = slice(start, start + size)
        main, rest = dot(high_ref[at, :], weight), dot(mid_ref[at, :], weight)
        value = main[:, :BLOCK] + (main[:, BLOCK:] + (rest[:, :BLOCK] + rest[:, BLOCK:]))
        basis_ref[:, at] = value.T[:RANK, :]


def tree(parts):
    while len(parts) > 1:
        parts = [parts[i] + parts[i + 1] for i in range(0, len(parts), 2)]
    return parts[0]


def everyone(value, axis, size):
    return lax.all_to_all(jnp.broadcast_to(value, (size,) + value.shape), axis, 0, 0)


def pick(pair, i):
    size = (1,) + pair.shape[1:]
    return lax.dynamic_slice(pair, (i, np.int32(0), np.int32(0)), size, allow_negative_indices=False)[0]


def stacked_sum(values):
    return tree([values[i] for i in range(values.shape[0])])


def total(flat, mine, theirs, low_core):
    swap = [(0, 1), (1, 0)]
    pair = flat.reshape(2, FLAT // 2, BLOCK)
    value = pick(pair, mine) + lax.ppermute(pick(pair, theirs), "core", swap)
    value = stacked_sum(lax.all_to_all(value.reshape(SX, -1, BLOCK), "x", 0, 0))
    value = stacked_sum(lax.all_to_all(value.reshape(SY, -1, BLOCK), "y", 0, 0))
    value = stacked_sum(everyone(value, "z", SZ))
    value = everyone(value, "y", SY).reshape(-1, BLOCK)
    value = everyone(value, "x", SX).reshape(-1, BLOCK)
    other = lax.ppermute(value, "core", swap)
    low = jnp.where(low_core, value, other)
    high = jnp.where(low_core, other, value)
    return jnp.concatenate([low, high])


def local(embeddings, test_matrix):
    rows = embeddings.shape[0]
    factor = float(np.sqrt(np.float32(rows * 2 * SX * SY * SZ)))
    core = lax.axis_index("core")
    embeddings, *where = lax.optimization_barrier((embeddings, core, 1 - core, core == 0))
    held = CHUNKS[-1][0] + (CHUNKS[-1][1] + 127) // 128 * 128
    flat, high, mid = pl.pallas_call(
        gram_kernel,
        in_specs=[pl.BlockSpec(memory_space=pl.ANY)],
        out_specs=[pl.BlockSpec(memory_space=pltpu.VMEM)] * 3,
        out_shape=[jax.ShapeDtypeStruct((FLAT, BLOCK), jnp.float32)] + [jax.ShapeDtypeStruct((held, D), jnp.bfloat16)] * 2,
        scratch_shapes=[pltpu.VMEM((rows, D), jnp.float32)]
        + [pltpu.VMEM((9, 256, 256), jnp.float32)] * 2
        + [pltpu.SemaphoreType.DMA((len(CHUNKS),))],
        compiler_params=pltpu.CompilerParams(vmem_limit_bytes=LIMITS[0]),
        cost_estimate=pl.CostEstimate(flops=2 * rows * D * D * 2, bytes_accessed=4 * rows * D, transcendentals=0),
    )(embeddings)
    flat = total(flat, *where)
    basis, projected = pl.pallas_call(
        lambda *refs: finish_kernel(factor, *refs),
        in_specs=[pl.BlockSpec(memory_space=pltpu.VMEM)] * 4,
        out_specs=[pl.BlockSpec(memory_space=pltpu.VMEM)] * 2,
        out_shape=[jax.ShapeDtypeStruct((RANK, rows), jnp.float32), jax.ShapeDtypeStruct((RANK, D), jnp.float32)],
        scratch_shapes=[pltpu.VMEM((3, D, D), jnp.bfloat16)],
        compiler_params=pltpu.CompilerParams(vmem_limit_bytes=LIMITS[1]),
        cost_estimate=pl.CostEstimate(flops=2 * rows * D * RANK * 8, bytes_accessed=4 * rows * D, transcendentals=0),
    )(flat, jnp.pad(test_matrix.T, ((0, 8), (0, 0))), high, mid)
    return basis.T, projected


def solution(mesh):
    grid = Mesh(mesh.devices.reshape(SX, SY, SZ, 2), ("x", "y", "z", "core"))
    in_specs = (P(("x", "y", "z", "core"), None), P())
    out_specs = (P(("x", "y", "z", "core"), None), P())
    return jax.shard_map(local, mesh=grid, in_specs=in_specs, out_specs=out_specs, check_vma=False)
```

```python
import jax
import jax.numpy as jnp
import numpy as np
from jax import lax
from jax.experimental import pallas as pl
from jax.experimental.pallas import tpu as pltpu
from jax.sharding import Mesh, PartitionSpec as P

SX, SY, SZ = 4, 8, 8
D, RANK = 768, 80
BLOCK = 128
NB = D // BLOCK
UPPER = [(a, b) for a in range(NB) for b in range(a + 1, NB)]
PACKED = len(UPPER) * BLOCK
DIAGS = PACKED + NB // 2 * BLOCK
FLAT = 2368
CHUNKS = ((0, 256), (256, 512), (768, 576))
LIMITS = 45 * 2 ** 20, 45 * 2 ** 20


def split(value):
    high = value.astype(jnp.bfloat16)
    rest = value - high.astype(jnp.float32)
    mid = rest.astype(jnp.bfloat16)
    low = (rest - mid.astype(jnp.float32)).astype(jnp.bfloat16)
    return high, mid, low


def halves(value):
    high = value.astype(jnp.bfloat16)
    return high, (value - high.astype(jnp.float32)).astype(jnp.bfloat16)


def dot(left, right, dim=0):
    return lax.dot_general(left, right, (((1,), (dim,)), ((), ())), preferred_element_type=jnp.float32)


def iota(axis):
    return lax.broadcasted_iota(jnp.int32, (BLOCK, BLOCK), axis)


def gram_kernel(x_hbm, flat_ref, high_ref, mid_ref, x_ref, even_ref, odd_ref, sem):
    copies = []
    for n, (start, size) in enumerate(CHUNKS):
        at = pl.ds(start, size)
        copies.append(pltpu.make_async_copy(x_hbm.at[at, :], x_ref.at[at, :], sem.at[n]))
        copies[-1].start()
    used = x_ref.shape[0]
    for ref in (high_ref, mid_ref):
        ref[used:, :] = jnp.zeros((ref.shape[0] - used, D), jnp.bfloat16)

    def arrive(n):
        start, size = CHUNKS[n]
        copies[n].wait()
        at = slice(start, start + size)
        high_ref[at, :], mid_ref[at, :] = halves(x_ref[at, :])

    arrive(0)
    for n, (start, size) in enumerate(CHUNKS):
        deep = slice(start, start + (size + 127) // 128 * 128)
        for i in range(3):
            high_t = high_ref[deep, 256 * i:256 * (i + 1)].T
            for j in range(3):
                cols = slice(256 * j, 256 * (j + 1))
                if i <= j:
                    value = dot(high_t, high_ref[deep, cols])
                    even_ref[3 * i + j] = value if n == 0 else even_ref[3 * i + j] + value
                value = dot(high_t, mid_ref[deep, cols])
                odd_ref[3 * i + j] = value if n == 0 else odd_ref[3 * i + j] + value
            if i == 0 and n + 1 < len(CHUNKS):
                arrive(n + 1)

    row, col = iota(0), iota(1)
    flat_ref[DIAGS:, :] = jnp.zeros((FLAT - DIAGS, BLOCK), jnp.float32)
    for i in range(3):
        for j in range(i, 3):
            value = even_ref[3 * i + j] + (odd_ref[3 * i + j] + odd_ref[3 * j + i].T)
            for p in range(2):
                for q in range(2):
                    a, b = 2 * i + p, 2 * j + q
                    if a < b:
                        at = UPPER.index((a, b)) * BLOCK
                        flat_ref[at:at + BLOCK, :] = value[p * BLOCK:(p + 1) * BLOCK, q * BLOCK:(q + 1) * BLOCK]
            if i == j:
                first, second = value[:BLOCK, :BLOCK], value[BLOCK:, BLOCK:]
                at = PACKED + i * BLOCK
                flat_ref[at:at + BLOCK, :] = jnp.where(row <= col, first, second)
                flat_ref[DIAGS + i:DIAGS + i + 1, :] = jnp.sum(jnp.where(row == col, second, 0.0), axis=0, keepdims=True)


def inverse_factor(gram):
    groups, shape = RANK // 8, (8, RANK)
    lane = lax.broadcasted_iota(jnp.int32, shape, 1)
    sub = lax.broadcasted_iota(jnp.int32, shape, 0)
    state = [gram[8 * g:8 * g + 8, :] for g in range(groups)]
    diagonal = [jnp.where(lane == 8 * g + sub, state[g], 0.0) for g in range(groups)]
    along = lax.rsqrt(jnp.sum(sum(diagonal[1:], diagonal[0]), axis=0, keepdims=True))
    state = [state[g] * lax.rsqrt(jnp.sum(diagonal[g], axis=1, keepdims=True)) * along for g in range(groups)]

    def column(h, j):
        return jnp.broadcast_to(state[h][:, j:j + 1], shape)

    def line(value, i):
        return jnp.broadcast_to(value[i:i + 1, :], shape)

    scales = []
    coming = [column(0, k) for k in range(8)]
    for g in range(groups):
        at = 8 * g
        head = coming
        own, pivots, steps = state[g], None, []
        for k in range(0, 8, 2):
            u, v = head[k], head[k + 1]
            a, b, c = line(u, k), line(v, k), line(v, k + 1)
            inverse = 1.0 / (a * c - b * b)
            rest = sub > k + 1
            first = jnp.where(rest, u * c - v * b, 0.0) * inverse
            second = jnp.where(rest, v * a - u * b, 0.0) * inverse
            here, there = lane == at + k, lane == at + k + 1
            rows = (jnp.where(here, 1.0, jnp.where(there, 0.0, line(own, k))),
                    jnp.where(here, 0.0, jnp.where(there, 1.0, line(own, k + 1))))
            pairs = {m: (line(head[m], k), line(head[m], k + 1)) for m in range(k + 2, 8)}
            for m in range(k + 2, 8):
                head[m] = head[m] - (first * pairs[m][0] + second * pairs[m][1])
            own = jnp.where(rest & (here | there), 0.0, own) - (first * rows[0] + second * rows[1])
            ratio = b / a
            own = jnp.where(sub == k + 1, rows[1] - ratio * rows[0], own)
            pivots = a if k == 0 else jnp.where(sub >= k, a, pivots)
            pivots = jnp.where(sub > k, c - b * ratio, pivots)
            later = (lane > at + k + 1) & (lane < at + 8)
            rows = [jnp.where(later, 0.0, row) for row in rows]
            steps.append((k, c * inverse, b * inverse, a * inverse, rows, pairs))
        state[g] = own
        scales.append(lax.rsqrt(pivots))
        inside = (lane >= at) & (lane < at + 8)
        for h in range(g + 1, groups):
            below = [column(h, at + k) for k in range(8)]
            value = jnp.where(inside, 0.0, state[h])
            if h == g + 1:
                coming = [column(h, at + 8 + k) for k in range(8)]
            for k, p, q, r, rows, pairs in steps:
                u, v = below[k], below[k + 1]
                first, second = u * p - v * q, v * r - u * q
                if h == g + 1:
                    coming = [coming[m] - (first * line(u, m) + second * line(v, m)) for m in range(8)]
                for m in range(k + 2, 8):
                    below[m] = below[m] - (first * pairs[m][0] + second * pairs[m][1])
                value = value - (first * rows[0] + second * rows[1])
            state[h] = value
    result = []
    for g in range(groups):
        value = jnp.where(lane < 8 * g + sub, state[g], jnp.where(lane == 8 * g + sub, 1.0, 0.0))
        result.append(value * scales[g] * along)
    return jnp.concatenate(result, axis=0)


def stack(value):
    return jnp.concatenate(split(value), axis=0)


def times(stacked, parts, dim=0):
    high, mid, low = parts
    n = RANK
    first, second, third = dot(stacked, high, dim), dot(stacked[:2 * n], mid, dim), dot(stacked[:n], low, dim)
    small = first[2 * n:] + second[n:] + third
    return first[:n] + (first[n:2 * n] + second[:n] + small)


def finish_kernel(factor, flat_ref, test_ref, high_ref, mid_ref, basis_hbm, projected_hbm, basis_ref, projected_ref, c_ref, sem):
    row, col = iota(0), iota(1)

    def place(a, b, value):
        for k, part in enumerate(split(value)):
            c_ref[k, a * BLOCK:(a + 1) * BLOCK, b * BLOCK:(b + 1) * BLOCK] = part

    test = stack(test_ref[:RANK, :])
    image = None
    for i in range(NB // 2):
        for n, (a, b) in enumerate(UPPER):
            if a // 2 == i:
                value = flat_ref[n * BLOCK:(n + 1) * BLOCK, :]
                place(a, b, value)
                place(b, a, value.T)
        value = flat_ref[PACKED + i * BLOCK:PACKED + (i + 1) * BLOCK, :]
        flipped = value.T
        place(2 * i, 2 * i, jnp.where(row <= col, value, flipped))
        other = jnp.where(row > col, value, flipped)
        place(2 * i + 1, 2 * i + 1, jnp.where(row == col, flat_ref[DIAGS + i:DIAGS + i + 1, :], other))
        deep = slice(256 * i, 256 * (i + 1))
        value = times(test[:, deep], [c_ref[k, deep, :] for k in range(3)])
        image = value if i == 0 else image + value

    covariance = [c_ref.at[k] for k in range(3)]
    gram = times(test, split(image), 1)
    first = inverse_factor(gram)
    spanned = times(stack(first), split(image))
    spanned_stack = stack(spanned)
    reach = times(spanned_stack, [part[...] for part in covariance])
    gram = times(spanned_stack, split(reach), 1)
    second = inverse_factor(gram)
    second_stack = stack(second)
    projected_ref[...] = times(second_stack, split(reach)) * (1.0 / factor)
    copies = [pltpu.make_async_copy(projected_ref, projected_hbm, sem.at[0])]
    copies[0].start()
    empty = jnp.zeros((BLOCK - RANK, D), jnp.float32)
    weight = jnp.concatenate([times(second_stack, split(spanned)) * factor, empty], axis=0)
    weight = jnp.concatenate(halves(weight), axis=0).T
    total_rows = basis_ref.shape[1]
    for start in range(0, total_rows, 256):
        size = min(256, total_rows - start)
        at = slice(start, start + size)
        main, rest = dot(high_ref[at, :], weight), dot(mid_ref[at, :], weight)
        value = main[:, :BLOCK] + (main[:, BLOCK:] + (rest[:, :BLOCK] + rest[:, BLOCK:]))
        basis_ref[:, at] = value.T[:RANK, :]
        if start + size == total_rows or start == 512:
            piece = pl.ds(0, 768) if start == 512 else pl.ds(768, total_rows - 768)
            copies.append(pltpu.make_async_copy(basis_ref.at[:, piece], basis_hbm.at[:, piece], sem.at[len(copies)]))
            copies[-1].start()
    for copy in copies:
        copy.wait()


def tree(parts):
    while len(parts) > 1:
        parts = [parts[i] + parts[i + 1] for i in range(0, len(parts), 2)]
    return parts[0]


def everyone(value, axis, size):
    return lax.all_to_all(jnp.broadcast_to(value, (size,) + value.shape), axis, 0, 0)


def pick(pair, i):
    size = (1,) + pair.shape[1:]
    return lax.dynamic_slice(pair, (i, np.int32(0), np.int32(0)), size, allow_negative_indices=False)[0]


def stacked_sum(values):
    return tree([values[i] for i in range(values.shape[0])])


def total(flat, mine, theirs, low_core):
    swap = [(0, 1), (1, 0)]
    pair = flat.reshape(2, FLAT // 2, BLOCK)
    value = pick(pair, mine) + lax.ppermute(pick(pair, theirs), "core", swap)
    value = stacked_sum(lax.all_to_all(value.reshape(SX, -1, BLOCK), "x", 0, 0))
    rows = value.shape[0]
    value = jnp.pad(value, ((0, -rows % (8 * SY)), (0, 0)))
    value = stacked_sum(lax.all_to_all(value.reshape(SY, -1, BLOCK), "y", 0, 0))
    value = stacked_sum(everyone(value, "z", SZ))
    value = everyone(value, "y", SY).reshape(-1, BLOCK)[:rows]
    value = everyone(value, "x", SX).reshape(-1, BLOCK)
    other = lax.ppermute(value, "core", swap)
    low = jnp.where(low_core, value, other)
    high = jnp.where(low_core, other, value)
    return jnp.concatenate([low, high])


def local(embeddings, test_matrix):
    rows = embeddings.shape[0]
    factor = float(np.sqrt(np.float32(rows * 2 * SX * SY * SZ)))
    core = lax.axis_index("core")
    embeddings, *where = lax.optimization_barrier((embeddings, core, 1 - core, core == 0))
    held = CHUNKS[-1][0] + (CHUNKS[-1][1] + 127) // 128 * 128
    flat, high, mid = pl.pallas_call(
        gram_kernel,
        in_specs=[pl.BlockSpec(memory_space=pl.ANY)],
        out_specs=[pl.BlockSpec(memory_space=pltpu.VMEM)] * 3,
        out_shape=[jax.ShapeDtypeStruct((FLAT, BLOCK), jnp.float32)] + [jax.ShapeDtypeStruct((held, D), jnp.bfloat16)] * 2,
        scratch_shapes=[pltpu.VMEM((rows, D), jnp.float32)]
        + [pltpu.VMEM((9, 256, 256), jnp.float32)] * 2
        + [pltpu.SemaphoreType.DMA((len(CHUNKS),))],
        compiler_params=pltpu.CompilerParams(vmem_limit_bytes=LIMITS[0]),
        cost_estimate=pl.CostEstimate(flops=2 * rows * D * D * 2, bytes_accessed=4 * rows * D, transcendentals=0),
    )(embeddings)
    flat = total(flat, *where)
    basis, projected = pl.pallas_call(
        lambda *refs: finish_kernel(factor, *refs),
        in_specs=[pl.BlockSpec(memory_space=pltpu.VMEM)] * 4,
        out_specs=[pl.BlockSpec(memory_space=pl.ANY)] * 2,
        out_shape=[jax.ShapeDtypeStruct((RANK, rows), jnp.float32), jax.ShapeDtypeStruct((RANK, D), jnp.float32)],
        scratch_shapes=[
            pltpu.VMEM((RANK, rows), jnp.float32),
            pltpu.VMEM((RANK, D), jnp.float32),
            pltpu.VMEM((3, D, D), jnp.bfloat16),
            pltpu.SemaphoreType.DMA((3,)),
        ],
        compiler_params=pltpu.CompilerParams(vmem_limit_bytes=LIMITS[1]),
        cost_estimate=pl.CostEstimate(flops=2 * rows * D * RANK * 8, bytes_accessed=4 * rows * D, transcendentals=0),
    )(flat, jnp.pad(test_matrix.T, ((0, 8), (0, 0))), high, mid)
    return basis.T, projected


def solution(mesh):
    grid = Mesh(mesh.devices.reshape(SX, SY, SZ, 2), ("x", "y", "z", "core"))
    in_specs = (P(("x", "y", "z", "core"), None), P())
    out_specs = (P(("x", "y", "z", "core"), None), P())
    return jax.shard_map(local, mesh=grid, in_specs=in_specs, out_specs=out_specs, check_vma=False)
```

```python
import jax
import jax.numpy as jnp
import numpy as np
from jax import lax
from jax.experimental import pallas as pl
from jax.experimental.pallas import tpu as pltpu
from jax.sharding import Mesh, PartitionSpec as P

SX, SY, SZ = 4, 8, 8
D, RANK = 768, 80
BLOCK = 128
NB = D // BLOCK
UPPER = [(a, b) for a in range(NB) for b in range(a + 1, NB)]
PACKED = len(UPPER) * BLOCK
DIAGS = PACKED + NB // 2 * BLOCK
FLAT = 2368
CHUNKS = ((0, 256), (256, 512), (768, 576))
LIMITS = 45 * 2 ** 20, 45 * 2 ** 20


def split(value):
    high = value.astype(jnp.bfloat16)
    rest = value - high.astype(jnp.float32)
    mid = rest.astype(jnp.bfloat16)
    low = (rest - mid.astype(jnp.float32)).astype(jnp.bfloat16)
    return high, mid, low


def halves(value):
    high = value.astype(jnp.bfloat16)
    return high, (value - high.astype(jnp.float32)).astype(jnp.bfloat16)


def dot(left, right, dim=0):
    return lax.dot_general(left, right, (((1,), (dim,)), ((), ())), preferred_element_type=jnp.float32)


def iota(axis):
    return lax.broadcasted_iota(jnp.int32, (BLOCK, BLOCK), axis)


def gram_kernel(x_hbm, flat_ref, high_ref, mid_ref, x_ref, even_ref, odd_ref, sem):
    copies = []
    for n, (start, size) in enumerate(CHUNKS):
        at = pl.ds(start, size)
        copies.append(pltpu.make_async_copy(x_hbm.at[at, :], x_ref.at[at, :], sem.at[n]))
        copies[-1].start()
    used = x_ref.shape[0]
    for ref in (high_ref, mid_ref):
        ref[used:, :] = jnp.zeros((ref.shape[0] - used, D), jnp.bfloat16)

    def arrive(n):
        start, size = CHUNKS[n]
        copies[n].wait()
        at = slice(start, start + size)
        high_ref[at, :], mid_ref[at, :] = halves(x_ref[at, :])

    arrive(0)
    for n, (start, size) in enumerate(CHUNKS):
        deep = slice(start, start + (size + 127) // 128 * 128)
        for i in range(3):
            high_t = high_ref[deep, 256 * i:256 * (i + 1)].T
            cols = slice(256 * i, D)
            value = dot(high_t, high_ref[deep, cols])
            even_ref[i, :, cols] = value if n == 0 else even_ref[i, :, cols] + value
            value = dot(high_t, mid_ref[deep, :])
            odd_ref[i] = value if n == 0 else odd_ref[i] + value
            if i == 0 and n + 1 < len(CHUNKS):
                arrive(n + 1)

    row, col = iota(0), iota(1)
    flat_ref[DIAGS:, :] = jnp.zeros((FLAT - DIAGS, BLOCK), jnp.float32)
    for i in range(3):
        for j in range(i, 3):
            left, right = slice(256 * i, 256 * (i + 1)), slice(256 * j, 256 * (j + 1))
            value = even_ref[i, :, right] + (odd_ref[i, :, right] + odd_ref[j, :, left].T)
            for p in range(2):
                for q in range(2):
                    a, b = 2 * i + p, 2 * j + q
                    if a < b:
                        at = UPPER.index((a, b)) * BLOCK
                        flat_ref[at:at + BLOCK, :] = value[p * BLOCK:(p + 1) * BLOCK, q * BLOCK:(q + 1) * BLOCK]
            if i == j:
                first, second = value[:BLOCK, :BLOCK], value[BLOCK:, BLOCK:]
                at = PACKED + i * BLOCK
                flat_ref[at:at + BLOCK, :] = jnp.where(row <= col, first, second)
                flat_ref[DIAGS + i:DIAGS + i + 1, :] = jnp.sum(jnp.where(row == col, second, 0.0), axis=0, keepdims=True)


def inverse_factor(gram):
    groups, shape = RANK // 8, (8, RANK)
    lane = lax.broadcasted_iota(jnp.int32, shape, 1)
    sub = lax.broadcasted_iota(jnp.int32, shape, 0)
    state = [gram[8 * g:8 * g + 8, :] for g in range(groups)]
    diagonal = [jnp.where(lane == 8 * g + sub, state[g], 0.0) for g in range(groups)]
    along = lax.rsqrt(jnp.sum(sum(diagonal[1:], diagonal[0]), axis=0, keepdims=True))
    state = [state[g] * lax.rsqrt(jnp.sum(diagonal[g], axis=1, keepdims=True)) * along for g in range(groups)]

    def column(h, j):
        return jnp.broadcast_to(state[h][:, j:j + 1], shape)

    def line(value, i):
        return jnp.broadcast_to(value[i:i + 1, :], shape)

    scales = []
    coming = [column(0, k) for k in range(8)]
    for g in range(groups):
        at = 8 * g
        head = coming
        own, pivots, steps = state[g], None, []
        for k in range(0, 8, 2):
            u, v = head[k], head[k + 1]
            a, b, c = line(u, k), line(v, k), line(v, k + 1)
            inverse = 1.0 / (a * c - b * b)
            rest = sub > k + 1
            first = jnp.where(rest, u * c - v * b, 0.0) * inverse
            second = jnp.where(rest, v * a - u * b, 0.0) * inverse
            here, there = lane == at + k, lane == at + k + 1
            rows = (jnp.where(here, 1.0, jnp.where(there, 0.0, line(own, k))),
                    jnp.where(here, 0.0, jnp.where(there, 1.0, line(own, k + 1))))
            pairs = {m: (line(head[m], k), line(head[m], k + 1)) for m in range(k + 2, 8)}
            for m in range(k + 2, 8):
                head[m] = head[m] - (first * pairs[m][0] + second * pairs[m][1])
            own = jnp.where(rest & (here | there), 0.0, own) - (first * rows[0] + second * rows[1])
            ratio = b / a
            own = jnp.where(sub == k + 1, rows[1] - ratio * rows[0], own)
            pivots = a if k == 0 else jnp.where(sub >= k, a, pivots)
            pivots = jnp.where(sub > k, c - b * ratio, pivots)
            later = (lane > at + k + 1) & (lane < at + 8)
            rows = [jnp.where(later, 0.0, row) for row in rows]
            steps.append((k, c * inverse, b * inverse, a * inverse, rows, pairs))
        state[g] = own
        scales.append(lax.rsqrt(pivots))
        inside = (lane >= at) & (lane < at + 8)
        for h in range(g + 1, groups):
            below = [column(h, at + k) for k in range(8)]
            value = jnp.where(inside, 0.0, state[h])
            if h == g + 1:
                coming = [column(h, at + 8 + k) for k in range(8)]
            for k, p, q, r, rows, pairs in steps:
                u, v = below[k], below[k + 1]
                first, second = u * p - v * q, v * r - u * q
                if h == g + 1:
                    coming = [coming[m] - (first * line(u, m) + second * line(v, m)) for m in range(8)]
                for m in range(k + 2, 8):
                    below[m] = below[m] - (first * pairs[m][0] + second * pairs[m][1])
                value = value - (first * rows[0] + second * rows[1])
            state[h] = value
    result = []
    for g in range(groups):
        value = jnp.where(lane < 8 * g + sub, state[g], jnp.where(lane == 8 * g + sub, 1.0, 0.0))
        result.append(value * scales[g] * along)
    return jnp.concatenate(result, axis=0)


def stack(value):
    return jnp.concatenate(split(value), axis=0)


def times(stacked, parts, dim=0):
    high, mid, low = parts
    n = RANK
    first, second, third = dot(stacked, high, dim), dot(stacked[:2 * n], mid, dim), dot(stacked[:n], low, dim)
    small = first[2 * n:] + second[n:] + third
    return first[:n] + (first[n:2 * n] + second[:n] + small)


def finish_kernel(factor, low_ref, upper_ref, test_ref, high_ref, mid_ref, basis_hbm, projected_hbm, basis_ref, projected_ref, c_ref, sem):
    row, col = iota(0), iota(1)

    def flat(start, size):
        end, middle = start + size, FLAT // 2
        if end <= middle:
            return low_ref[start:end, :]
        if start >= middle:
            return upper_ref[start - middle:end - middle, :]
        return jnp.concatenate([low_ref[start:, :], upper_ref[:end - middle, :]], axis=0)

    def place(a, b, value):
        for k, part in enumerate(split(value)):
            c_ref[k, a * BLOCK:(a + 1) * BLOCK, b * BLOCK:(b + 1) * BLOCK] = part

    test = stack(test_ref[:RANK, :])
    image = None
    for i in range(NB // 2):
        for n, (a, b) in enumerate(UPPER):
            if a // 2 == i:
                value = flat(n * BLOCK, BLOCK)
                place(a, b, value)
                place(b, a, value.T)
        value = flat(PACKED + i * BLOCK, BLOCK)
        flipped = value.T
        place(2 * i, 2 * i, jnp.where(row <= col, value, flipped))
        other = jnp.where(row > col, value, flipped)
        place(2 * i + 1, 2 * i + 1, jnp.where(row == col, flat(DIAGS + i, 1), other))
        deep = slice(256 * i, 256 * (i + 1))
        value = times(test[:, deep], [c_ref[k, deep, :] for k in range(3)])
        image = value if i == 0 else image + value

    covariance = [c_ref.at[k] for k in range(3)]
    gram = times(test, split(image), 1)
    first = inverse_factor(gram)
    spanned = times(stack(first), split(image))
    spanned_stack = stack(spanned)
    reach = times(spanned_stack, [part[...] for part in covariance])
    gram = times(spanned_stack, split(reach), 1)
    second = inverse_factor(gram)
    second_stack = stack(second)
    projected_ref[...] = times(second_stack, split(reach)) * (1.0 / factor)
    copies = [pltpu.make_async_copy(projected_ref, projected_hbm, sem.at[0])]
    copies[0].start()
    empty = jnp.zeros((BLOCK - RANK, D), jnp.float32)
    weight = jnp.concatenate([times(second_stack, split(spanned)) * factor, empty], axis=0)
    weight = jnp.concatenate(halves(weight), axis=0).T
    total_rows = basis_ref.shape[1]
    for start in range(0, total_rows, 256):
        size = min(256, total_rows - start)
        at = slice(start, start + size)
        main, rest = dot(high_ref[at, :], weight), dot(mid_ref[at, :], weight)
        value = main[:, :BLOCK] + (main[:, BLOCK:] + (rest[:, :BLOCK] + rest[:, BLOCK:]))
        basis_ref[:, at] = value.T[:RANK, :]
        if start + size == total_rows or start == 512:
            piece = pl.ds(0, 768) if start == 512 else pl.ds(768, total_rows - 768)
            copies.append(pltpu.make_async_copy(basis_ref.at[:, piece], basis_hbm.at[:, piece], sem.at[len(copies)]))
            copies[-1].start()
    for copy in copies:
        copy.wait()


def tree(parts):
    while len(parts) > 1:
        parts = [parts[i] + parts[i + 1] for i in range(0, len(parts), 2)]
    return parts[0]


def everyone(value, axis, size):
    return lax.all_to_all(jnp.broadcast_to(value, (size,) + value.shape), axis, 0, 0)


def pick(pair, i):
    size = (1,) + pair.shape[1:]
    return lax.dynamic_slice(pair, (i, np.int32(0), np.int32(0)), size, allow_negative_indices=False)[0]


def stacked_sum(values):
    return tree([values[i] for i in range(values.shape[0])])


def total(flat, mine, theirs, low_core):
    swap = [(0, 1), (1, 0)]
    pair = flat.reshape(2, FLAT // 2, BLOCK)
    value = pick(pair, mine) + lax.ppermute(pick(pair, theirs), "core", swap)
    value = stacked_sum(lax.all_to_all(value.reshape(SX, -1, BLOCK), "x", 0, 0))
    rows = value.shape[0]
    value = jnp.pad(value, ((0, -rows % (8 * SY)), (0, 0)))
    value = stacked_sum(lax.all_to_all(value.reshape(SY, -1, BLOCK), "y", 0, 0))
    value = stacked_sum(everyone(value, "z", SZ))
    value = everyone(value, "y", SY).reshape(-1, BLOCK)[:rows]
    value = everyone(value, "x", SX).reshape(-1, BLOCK)
    other = lax.ppermute(value, "core", swap)
    low = jnp.where(low_core, value, other)
    high = jnp.where(low_core, other, value)
    return low, high


def local(embeddings, test_matrix):
    rows = embeddings.shape[0]
    factor = float(np.sqrt(np.float32(rows * 2 * SX * SY * SZ)))
    core = lax.axis_index("core")
    embeddings, *where = lax.optimization_barrier((embeddings, core, 1 - core, core == 0))
    held = CHUNKS[-1][0] + (CHUNKS[-1][1] + 127) // 128 * 128
    flat, high, mid = pl.pallas_call(
        gram_kernel,
        in_specs=[pl.BlockSpec(memory_space=pl.ANY)],
        out_specs=[pl.BlockSpec(memory_space=pltpu.VMEM)] * 3,
        out_shape=[jax.ShapeDtypeStruct((FLAT, BLOCK), jnp.float32)] + [jax.ShapeDtypeStruct((held, D), jnp.bfloat16)] * 2,
        scratch_shapes=[pltpu.VMEM((rows, D), jnp.float32)]
        + [pltpu.VMEM((3, 256, D), jnp.float32)] * 2
        + [pltpu.SemaphoreType.DMA((len(CHUNKS),))],
        compiler_params=pltpu.CompilerParams(vmem_limit_bytes=LIMITS[0]),
        cost_estimate=pl.CostEstimate(flops=2 * rows * D * D * 2, bytes_accessed=4 * rows * D, transcendentals=0),
    )(embeddings)
    low, upper = total(flat, *where)
    basis, projected = pl.pallas_call(
        lambda *refs: finish_kernel(factor, *refs),
        in_specs=[pl.BlockSpec(memory_space=pltpu.VMEM)] * 5,
        out_specs=[pl.BlockSpec(memory_space=pl.ANY)] * 2,
        out_shape=[jax.ShapeDtypeStruct((RANK, rows), jnp.float32), jax.ShapeDtypeStruct((RANK, D), jnp.float32)],
        scratch_shapes=[
            pltpu.VMEM((RANK, rows), jnp.float32),
            pltpu.VMEM((RANK, D), jnp.float32),
            pltpu.VMEM((3, D, D), jnp.bfloat16),
            pltpu.SemaphoreType.DMA((3,)),
        ],
        compiler_params=pltpu.CompilerParams(vmem_limit_bytes=LIMITS[1]),
        cost_estimate=pl.CostEstimate(flops=2 * rows * D * RANK * 8, bytes_accessed=4 * rows * D, transcendentals=0),
    )(low, upper, jnp.pad(test_matrix.T, ((0, 8), (0, 0))), high, mid)
    return basis.T, projected


def solution(mesh):
    grid = Mesh(mesh.devices.reshape(SX, SY, SZ, 2), ("x", "y", "z", "core"))
    in_specs = (P(("x", "y", "z", "core"), None), P())
    out_specs = (P(("x", "y", "z", "core"), None), P())
    return jax.shard_map(local, mesh=grid, in_specs=in_specs, out_specs=out_specs, check_vma=False)
```
